512 devices in a mesh: cp: 16 (over y, x_hi, core), ep: 32 (over x_lo, z).
Axes of the slice: x: 4 (x_hi: 2, x_lo: 2; x = x_hi * 2 + x_lo), y: 4, z: 16, core: 2. Of those that a mesh axis runs over, the one named last changes fastest.
Arguments:
- query_act: bfloat16 [2048, 12288], P('cp', 'ep'), may hold values from -6 to 6
- key_act: bfloat16 [2048, 12288], P('cp', 'ep'), may hold values from -6 to 6
- value_act: bfloat16 [2048, 8192], P('cp', 'ep'), may hold values from -6 to 6
- out_grad: bfloat16 [2048, 8192], P('cp', 'ep'), may hold values from -24 to 24
- attn_out: bfloat16 [2048, 8192], P('cp', 'ep'), may hold values from -0.59765625 to 0.59765625
- log_norm: float32 [64, 2048], P('ep', 'cp'), may hold values from 0 to 20
- layer_grad: bfloat16 [2048, 7168], P('cp', 'ep'), may hold values from -6 to 6
- gate_probs: float32 [2048, 8], P('cp'), may hold values from 0.05 to 1
- expert_ids: int32 [2048, 8], P('cp'), may hold values from 0 to 31, all different within a row; in each aligned block of 128 rows (0 to 127, 128 to 255, ...) at most 64 rows name the same one
- hidden_acts: bfloat16 [32, 1024, 2048], P('ep', 'cp'), may hold values from -1.5 to 1.5
Outputs:
- query_grad: bfloat16 [2048, 12288], P('cp', 'ep')
- key_grad: bfloat16 [2048, 12288], P('cp', 'ep')
- value_grad: bfloat16 [2048, 8192], P('cp', 'ep')
- down_grad: bfloat16 [32, 2048, 7168], P('ep', None, 'cp')
The draws below stay inside these ranges and needn't reach their ends.
Inputs may be any that keep to these rules, and one draw needn't show every extreme that they name: `expert_ids`: in each aligned block of 128 rows (the rows of one index of cp), no expert is named by more than 64 rows, a bound that some block reaches; a row names 8 different experts.
All inputs are finite; a program needn't handle non-finite values.
Results may differ from the reference program's by a relative error of at most 0.0064.
Values may be sent and summed in bfloat16 or wider, within the bound.
A program may use at most 64 MiB of HBM per device.

```python
import math
import jax
import jax.numpy as jnp
import numpy as np
from jax import lax

D = 7168
F = 2048
TOP = 8
QK = 192
DH = 128
EXPERTS = 32
R = 128
CAP = 64
HEADS = 64
LEN = 2048
N_CP = 16


def draw_log_norm(key, part):
    key = jax.random.fold_in(key, 11)
    position = jnp.arange(LEN, dtype=jnp.float32)
    offset = jax.random.uniform(key, (HEADS, LEN), jnp.float32, 0.3, 0.8)
    return jnp.log(position + 1.0)[None, :] + offset


def block_levels(key, shape, pieces, low, top_value):
    factor_of, own = 1.0, jax.random.fold_in(key, 6)
    for dim, parts in pieces:
        heights = jnp.exp(jax.random.uniform(jax.random.fold_in(own, dim), (parts,), jnp.float32, low / len(pieces), top_value / len(pieces)))
        factor_of = factor_of * jnp.repeat(heights, shape[dim] // parts).reshape([-1 if axis == dim else 1 for axis in range(len(shape))])
    return factor_of


def shared_out(own_key, own, number, rows, number_of, top, limit, skew):
    order = jax.random.permutation(own_key, number_of)
    crowded, ordinary = portions_of(number_of, rows * top, limit, skew, True), portions_of(number_of, rows * top, limit, skew, False)
    places = jnp.arange(number_of)

    def named(lengths, offset_by):
        used = int((lengths > 0).sum())
        fixed = max(1, used // 4)
        shifted = fixed + (places - fixed + offset_by * (used - fixed)) % max(1, number_of - fixed)
        return jnp.zeros((number_of,), jnp.int32).at[order[jnp.where(places < fixed, places, shifted)]].set(jnp.asarray(lengths, jnp.int32))

    lengths = jnp.where(number % 4 == 0, named(crowded, number // 4), named(ordinary, number - number // 4 - 1))
    mixed = jax.random.permutation(jax.random.fold_in(own, 3), number_of)
    giver, receiver = mixed[0:number_of // 2 * 2:2], mixed[1:number_of // 2 * 2:2]
    margin = jnp.minimum(lengths[giver] - 1, limit - lengths[receiver]) // 2
    margin = jnp.where((giver == order[0]) | (receiver == order[0]) | (lengths[receiver] == 0), 0, jnp.maximum(margin, 0))
    shifted = jax.random.randint(jax.random.fold_in(own, 4), (number_of // 2,), 0, 1 << 20) % (margin + 1)
    lengths = lengths.at[giver].add(-shifted).at[receiver].add(shifted)
    items = jnp.searchsorted(jnp.cumsum(lengths), jnp.arange(rows * top), side="right").astype(jnp.int32)
    table = items.reshape(top, rows).T
    table = table[jax.random.permutation(jax.random.fold_in(own, 1), rows)]
    offset_by = jax.random.randint(jax.random.fold_in(own, 2), (rows, 1), 0, top)
    return jnp.take_along_axis(table, (jnp.arange(top)[None, :] + offset_by) % top, axis=1)


def portions_of(count, total, most, skew, full):
    portions = [(1 << 20) // math.isqrt(grade ** skew) + 1 for grade in range(1, count + 1)]
    largest = most if full else min(most, max(-(-total // count), total * portions[0] // sum(portions)))
    least = 1 if total - largest >= count - 1 else 0
    holding, rest = [largest] + [least] * (count - 1), total - largest - least * (count - 1)
    while rest > 0:
        free = [i for i in range(1, count) if holding[i] < largest] or [i for i in range(1, count) if holding[i] < most]
        mass, remaining = sum([portions[i] for i in free]), rest
        for i in free:
            extra = min(most - holding[i], max(1, remaining * portions[i] // mass), rest)
            holding[i] = holding[i] + extra
            rest = rest - extra
    return np.array(holding)


def noise(stream_key, shape, deviation, reach, split=(), kind=jnp.bfloat16):
    entries = deviation * jax.random.normal(stream_key, shape, jnp.float32)
    if split:
        entries = entries * block_levels(stream_key, shape, split, -0.22, 0.18)
    return jnp.clip(entries, -reach, reach).astype(kind)


def setup_inputs(seed: int = 0) -> dict:
    key_list = jax.random.split(jax.random.key(seed), 11)
    query_act = noise(key_list[0], (LEN, HEADS * QK), 1.0, 6.0, ((0, 16), (1, 32)))
    key_act = noise(key_list[1], (LEN, HEADS * QK), 1.0, 6.0, ((0, 16), (1, 32)))
    value_act = noise(key_list[2], (LEN, HEADS * DH), 1.0, 6.0, ((0, 16), (1, 32)))
    out_grad = noise(key_list[3], (LEN, HEADS * DH), 4.0, 24.0, ((0, 16), (1, 32)))
    attn_out = noise(key_list[4], (LEN, HEADS * DH), 0.1, 0.59765625, ((0, 16), (1, 32)))
    log_norm = draw_log_norm(jax.random.fold_in(key_list[10], 71), 0)
    layer_grad = noise(key_list[6], (LEN, D), 1.0, 6.0, ((0, 16), (1, 32)))
    gate_probs = jnp.clip(jnp.exp(math.log(1.0) - 2.9957323 * jax.random.uniform(key_list[7], (LEN, TOP), jnp.float32) ** block_levels(key_list[7], (LEN, TOP), ((0, 16),), -0.2, 0.2)), 0.05, 1.0)
    expert_ids_keys = jax.random.split(jax.random.fold_in(key_list[8], 1), LEN // R)
    expert_ids_turns = jax.random.permutation(jax.random.fold_in(key_list[8], 3), LEN // R)
    expert_ids = jax.vmap(lambda own, number: shared_out(jax.random.fold_in(key_list[8], 2), own, number, R, EXPERTS, TOP, CAP, 2))(expert_ids_keys, expert_ids_turns).reshape((LEN, TOP))
    hidden_acts = noise(key_list[9], (EXPERTS, N_CP * CAP, F), 0.25, 1.5, ((0, 32), (1, 16)))
    return dict(query_act=query_act, key_act=key_act, value_act=value_act, out_grad=out_grad, attn_out=attn_out, log_norm=log_norm, layer_grad=layer_grad, gate_probs=gate_probs, expert_ids=expert_ids, hidden_acts=hidden_acts)


HIGH = lax.Precision.HIGHEST

def head_grads(operands):
    q_head, k_head, v_head, do_head, delta_head, norm_head = operands
    scale = QK ** (-0.5)
    length = q_head.shape[0]
    position = jnp.arange(length)
    causal = position[:, None] >= position[None, :]
    scores = scale * jnp.dot(q_head, k_head.T, precision=HIGH)
    probs = jnp.where(causal, jnp.exp(scores - norm_head[:, None]), 0.0)
    dprobs = jnp.dot(do_head, v_head.T, precision=HIGH)
    dscores = lax.optimization_barrier((probs * (dprobs - delta_head[:, None])).astype(jnp.bfloat16)).astype(jnp.float32)
    probs_low = lax.optimization_barrier(probs.astype(jnp.bfloat16)).astype(jnp.float32)
    value_part = jnp.dot(probs_low.T, do_head, precision=HIGH)
    key_part = scale * jnp.dot(dscores.T, q_head, precision=HIGH)
    query_part = scale * jnp.dot(dscores, k_head, precision=HIGH)
    return (query_part, key_part, value_part)

def split_heads(array, width):
    return jnp.transpose(array.astype(jnp.float32).reshape(LEN, HEADS, width), (1, 0, 2))

def join_heads(array, width):
    return jnp.transpose(array, (1, 0, 2)).reshape(LEN, HEADS * width).astype(jnp.bfloat16)

def dispatch_block(operands):
    grad_rows, probs, ids = operands
    flat = ids.reshape(-1).astype(jnp.int32)
    onehot = (flat[:, None] == jnp.arange(EXPERTS, dtype=jnp.int32)[None, :]).astype(jnp.int32)
    before = jnp.cumsum(onehot, axis=0) - onehot
    slot = lax.optimization_barrier(jnp.sum(before * onehot, axis=1))
    target = (flat * CAP + slot).astype(jnp.int32)
    slot_rows = (probs[:, :, None] * grad_rows[:, None, :].astype(jnp.float32)).astype(jnp.bfloat16)
    slot_rows = slot_rows.reshape(flat.shape[0], D)
    buffer = jnp.zeros((EXPERTS * CAP, D), slot_rows.dtype).at[target].set(slot_rows)
    return buffer.reshape(EXPERTS, CAP, D)

def expert_grad(operands):
    hidden_one, buffer_one = operands
    flat = buffer_one.reshape(N_CP * CAP, D)
    return jnp.dot(hidden_one.T, flat, preferred_element_type=jnp.float32).astype(jnp.bfloat16)

def reference(query_act, key_act, value_act, out_grad, attn_out, log_norm, layer_grad, gate_probs, expert_ids, hidden_acts):
    q_heads = split_heads(query_act, QK)
    k_heads = split_heads(key_act, QK)
    v_heads = split_heads(value_act, DH)
    do_heads = split_heads(out_grad, DH)
    out_heads = split_heads(attn_out, DH)
    delta = lax.optimization_barrier(jnp.sum(do_heads * out_heads, axis=2))
    query_part, key_part, value_part = lax.map(head_grads, (q_heads, k_heads, v_heads, do_heads, delta, log_norm))
    query_grad = join_heads(query_part, QK)
    key_grad = join_heads(key_part, QK)
    value_grad = join_heads(value_part, DH)
    blocks = (layer_grad.reshape(N_CP, R, D), gate_probs.reshape(N_CP, R, TOP), expert_ids.reshape(N_CP, R, TOP))
    buffers = lax.map(dispatch_block, blocks)
    by_expert = jnp.swapaxes(buffers, 0, 1)
    down_grad = lax.map(expert_grad, (hidden_acts, by_expert))
    return (query_grad, key_grad, value_grad, down_grad)
```

```python
import jax
import jax.numpy as jnp
from jax import lax
from jax.experimental import pallas as pl
from jax.experimental.pallas import tpu as pltpu
from jax.sharding import PartitionSpec as P

QK = 192
DH = 128
CAP = 64
SCALE = QK ** (-0.5)
MESH = pl.DeviceIdType.MESH
F32 = jnp.float32
BF16 = jnp.bfloat16


def dot_nn(a, b):
    return lax.dot_general(a, b, (((1,), (0,)), ((), ())), preferred_element_type=F32)


def dot_nt(a, b):
    return lax.dot_general(a, b, (((1,), (1,)), ((), ())), preferred_element_type=F32)


def dot_tn(a, b):
    return lax.dot_general(a, b, (((0,), (0,)), ((), ())), preferred_element_type=F32)


def kernel(
    q_ref,
    k_ref,
    v_ref,
    do_ref,
    o_ref,
    ln_ref,
    lg_ref,
    gp_ref,
    id_ref,
    hid_ref,
    qg_ref,
    kg_ref,
    vg_ref,
    dg_ref,
    own_a,
    own_b,
    own_l,
    sw_a,
    sw_b,
    sw_l,
    ra,
    rb,
    rl,
    acc_a,
    acc_v,
    fo_a,
    fo_b,
    fi_a,
    fi_b,
    ring,
    send,
    cols,
    hid,
    sw_s,
    sw_r,
    at_s,
    at_r,
    fo_s,
    fo_r,
    rg_s,
    rg_r,
    cl_s,
    cl_r,
    loc_s,
    ho_s,
    ha_s,
    hb_s,
    hd_s,
    h_r,
):
    c = lax.axis_index("cp")
    e = lax.axis_index("ep")
    core = c % 2
    chip = c // 2
    z = e % 16
    xl = e // 16
    sib = c + 1 - 2 * core
    xpart = c + 2 - 4 * (chip % 2)

    def at_cp(other):
        return (other, e)

    def remote(src, dst, s_sem, r_sem, target):
        return pltpu.make_async_remote_copy(
            src_ref=src,
            dst_ref=dst,
            send_sem=s_sem,
            recv_sem=r_sem,
            device_id=target,
            device_id_type=MESH,
        )

    barrier = pltpu.get_barrier_semaphore()
    zup = xl * 16 + (z + 1) % 16
    zdown = xl * 16 + (z + 15) % 16
    cross = e + 16 - 32 * xl

    def greet_cp(n, carry):
        pl.semaphore_signal(barrier, inc=1, device_id=at_cp((c + n) % 16), device_id_type=MESH)
        return carry

    lax.fori_loop(1, 16, greet_cp, 0)
    pl.semaphore_signal(barrier, inc=1, device_id=(c, zup), device_id_type=MESH)
    pl.semaphore_signal(barrier, inc=1, device_id=(c, zdown), device_id_type=MESH)

    @pl.when(c // 8 != xl)
    def _():
        def greet_cross(n, carry):
            pl.semaphore_signal(barrier, inc=1, device_id=(n, cross), device_id_type=MESH)
            return carry

        lax.fori_loop(0, 16, greet_cross, 0)

    first = core == 0
    mine = pl.ds(pl.multiple_of(core * 128, 128), 128)

    def halves(ref, width):
        return ref[:, 0:width], ref[:, width : 2 * width]

    prod = do_ref[...].astype(F32) * o_ref[...].astype(F32)
    d0 = jnp.sum(prod[:, 0:DH], axis=1, keepdims=True)
    d1 = jnp.sum(prod[:, DH : 2 * DH], axis=1, keepdims=True)
    lane = lax.broadcasted_iota(jnp.int32, (128, 128), 1)
    both = jnp.where(lane == 0, d0, jnp.where(lane == 1, d1, 0.0))
    rows_d = both.T[0:8, :]
    rows_n = ln_ref[...]
    sub = lax.broadcasted_iota(jnp.int32, (8, 128), 0)
    l0 = jnp.where(sub == 0, rows_n[0:1, :], rows_d[0:1, :])
    l1 = jnp.where(sub == 0, rows_n[1:2, :], rows_d[1:2, :])
    own_l[core] = jnp.where(first, l0, l1)
    sw_l[...] = jnp.where(first, l1, l0)
    for n, ref in enumerate((q_ref, k_ref)):
        h0, h1 = halves(ref, QK)
        own_a[n, mine, :] = jnp.where(first, h0, h1)
        sw_a[n] = jnp.where(first, h1, h0)
    for n, ref in enumerate((do_ref, v_ref)):
        h0, h1 = halves(ref, DH)
        own_b[n, mine, :] = jnp.where(first, h0, h1)
        sw_b[n] = jnp.where(first, h1, h0)
    ring[z] = lg_ref[...]
    hid[c] = hid_ref[0]

    pl.semaphore_wait(barrier, 25)

    swaps = [
        remote(sw_a, own_a.at[:, mine, :], sw_s.at[0], sw_r.at[0], at_cp(sib)),
        remote(sw_b, own_b.at[:, mine, :], sw_s.at[1], sw_r.at[1], at_cp(sib)),
        remote(sw_l, own_l.at[core], sw_s.at[2], sw_r.at[2], at_cp(sib)),
    ]
    for copy in swaps:
        copy.start()

    def ring_copy(up, s):
        block = (z + 16 - s) % 16 if up else (z + s) % 16
        n = 0 if up else 1
        if isinstance(s, int) and s == 7:
            ref = ring.at[block, pl.ds(64 * n, 64), :]
        else:
            ref = ring.at[block]
        return remote(ref, ref, rg_s.at[n, s], rg_r.at[n, s], (c, zup if up else zdown))

    ring_copy(True, 0).start()
    ring_copy(False, 0).start()

    half_a, half_b = pl.ds(0, 32), pl.ds(32, 32)

    def ypeer(n):
        return (c + 4 * n) % 16

    def piece(owner, half):
        return hid.at[owner, half, :]

    def own_piece(n, target, half, col):
        return remote(
            piece(c, half), piece(c, half), ho_s.at[col, n], h_r.at[col, c], at_cp(target)
        )

    own_sends = [own_piece(0, xpart, half_a, 0)]
    own_sends += [own_piece(n, ypeer(n), half_b, 1) for n in (1, 3, 2)]
    for copy in own_sends:
        copy.start()
    for copy in swaps:
        copy.wait_recv()

    def att_copies(n):
        other = (c + 2 * n) % 16
        pick = jnp.where(other // 2 > chip, 1, 0)
        return (
            remote(own_a.at[pick], ra.at[chip], at_s.at[0, n], at_r.at[0, chip], at_cp(other)),
            remote(own_b.at[pick], rb.at[chip], at_s.at[1, n], at_r.at[1, chip], at_cp(other)),
            remote(own_l, rl.at[chip], at_s.at[2, n], at_r.at[2, chip], at_cp(other)),
        )

    def att_start(n, carry):
        for copy in att_copies(n):
            copy.start()
        return carry

    lax.fori_loop(1, 8, att_start, 0)
    later = [own_piece(n, ypeer(n), half_a, 0) for n in (1, 3, 2)]
    later.append(own_piece(0, xpart, half_b, 1))
    for copy in later:
        copy.start()
    own_sends += later
    whole = remote(hid.at[c], hid.at[c], ho_s.at[2, 0], h_r.at[2, c], at_cp(sib))
    whole.start()

    own_rows = own_l[...]
    norm_row = jnp.concatenate([own_rows[0, 0:1, :], own_rows[1, 0:1, :]], axis=1)
    delta_row = jnp.concatenate([own_rows[0, 1:2, :], own_rows[1, 1:2, :]], axis=1)
    col0 = jnp.concatenate([own_rows[0], jnp.zeros((120, 128), F32)], axis=0).T
    col1 = jnp.concatenate([own_rows[1], jnp.zeros((120, 128), F32)], axis=0).T
    norm_col = jnp.concatenate([col0[:, 0:1], col1[:, 0:1]], axis=0)
    delta_col = jnp.concatenate([col0[:, 1:2], col1[:, 1:2]], axis=0)

    def block(x, y, a, b, norm, delta, mask):
        probs = jnp.exp(SCALE * dot_nt(x, a) - norm)
        if mask is not None:
            probs = jnp.where(mask, probs, 0.0)
        ds = (probs * (dot_nt(y, b) - delta)).astype(BF16)
        return dot_nn(ds, a), dot_nn(probs.astype(BF16), b)

    r_iota = lax.broadcasted_iota(jnp.int32, (256, 256), 0)
    c_iota = lax.broadcasted_iota(jnp.int32, (256, 256), 1)
    q_part, _ = block(
        own_a[0], own_b[0], own_a[1], own_b[1], norm_col, delta_col, r_iota >= c_iota
    )
    k_part, v_part = block(
        own_a[1], own_b[1], own_a[0], own_b[0], norm_row, delta_row, c_iota >= r_iota
    )
    acc_a[0] = q_part
    acc_a[1] = k_part
    acc_v[0] = jnp.zeros((256, DH), F32)
    acc_v[1] = v_part

    def att_step(n):
        other = (chip + 8 - n) % 8
        for copy in (
            remote(own_a.at[0], ra.at[other], at_s.at[0, n], at_r.at[0, other], at_cp(sib)),
            remote(own_b.at[0], rb.at[other], at_s.at[1, n], at_r.at[1, other], at_cp(sib)),
            remote(own_l, rl.at[other], at_s.at[2, n], at_r.at[2, other], at_cp(sib)),
        ):
            copy.wait_recv()
        side = jnp.where(other > chip, 1, 0)
        rows = rl[other]
        far_norm = jnp.concatenate([rows[0, 0:1, :], rows[1, 0:1, :]], axis=1)
        far_delta = jnp.concatenate([rows[0, 1:2, :], rows[1, 1:2, :]], axis=1)
        is_far = other > chip
        norm = jnp.where(is_far, far_norm, norm_col)
        delta = jnp.where(is_far, far_delta, delta_col)
        part_a, part_v = block(
            own_a[side], own_b[side], ra[other], rb[other], norm, delta, None
        )
        acc_a[side] += part_a
        acc_v[side] += part_v

    def turn(n, carry):
        ring_copy(True, n - 1).wait_recv()
        ring_copy(True, n).start()
        ring_copy(False, n - 1).wait_recv()
        ring_copy(False, n).start()
        att_step(n)
        return carry

    def turn_ring(up, s):
        ring_copy(up, s).start()

    def arrived(owner, half, col):
        remote(piece(owner, half), piece(owner, half), hd_s.at[col, 0], h_r.at[col, owner], at_cp(sib)).wait_recv()

    def to_sibling(owner, half, col, n):
        return remote(
            piece(owner, half), piece(owner, half), hd_s.at[col, n], h_r.at[col, owner], at_cp(sib)
        )

    sib_sends = []
    fwd_sends = []
    lax.fori_loop(1, 2, turn, 0)
    arrived(xpart, half_a, 0)
    for n in (1, 3, 2):
        copy = remote(
            piece(xpart, half_a), piece(xpart, half_a), ha_s.at[n], h_r.at[0, xpart], at_cp(ypeer(n))
        )
        copy.start()
        fwd_sends.append(copy)
    sib_sends.append(to_sibling(xpart, half_a, 0, 0))
    sib_sends[-1].start()
    lax.fori_loop(2, 3, turn, 0)
    for n in (1, 3, 2):
        arrived(ypeer(n), half_b, 1)
        copy = remote(
            piece(ypeer(n), half_b), piece(ypeer(n), half_b), hb_s.at[n], h_r.at[1, ypeer(n)], at_cp(xpart)
        )
        copy.start()
        fwd_sends.append(copy)
        sib_sends.append(to_sibling(ypeer(n), half_b, 1, n))
        sib_sends[-1].start()
    lax.fori_loop(3, 7, turn, 0)
    ring_copy(True, 6).wait_recv()
    ring_copy(False, 6).wait_recv()
    ring_copy(True, 7).start()
    ring_copy(False, 7).start()
    att_step(7)

    ids = id_ref[...]
    gates = gp_ref[...]
    tri = (lax.broadcasted_iota(jnp.int32, (128, 128), 0) > lane).astype(BF16)
    table = jnp.zeros((128, 128), F32)
    weight = jnp.zeros((128, 128), F32)
    for n in range(2):
        hit = ids == 16 * n + z
        named = jnp.sum(jnp.where(hit, 1.0, 0.0), axis=1, keepdims=True)
        gate = jnp.sum(jnp.where(hit, gates, 0.0), axis=1, keepdims=True)
        before = dot_nn(tri, jnp.broadcast_to(named, (128, 128)).astype(BF16))
        place = before + (CAP * n)
        inside = (place == lane.astype(F32)) & (named > 0.5)
        table = jnp.where(inside, 1.0, table)
        weight = jnp.where(inside, gate, weight)
    onehot = table.T.astype(BF16)
    slot_gate = jnp.sum(weight.T, axis=1, keepdims=True)

    ring_copy(True, 7).wait_recv()
    ring_copy(False, 7).wait_recv()

    def col_target(k):
        return xl * 8 + k

    def col_copy(k, n):
        return remote(
            send.at[k, n], cols.at[c], cl_s.at[k, n], cl_r.at[c], (col_target(k), n * 16 + z)
        )

    def col_local(k, n):
        return pltpu.make_async_copy(send.at[k, n], cols.at[c], loc_s)

    def dispatch(k, carry):
        rows = jnp.concatenate([ring[2 * k], ring[2 * k + 1]], axis=1)
        out = (slot_gate * dot_nn(onehot, rows)).astype(BF16)
        for n in range(2):
            send[k, n] = out[n * CAP : (n + 1) * CAP, :]
            here = (col_target(k) == c) & (n == xl)

            @pl.when(here)
            def _():
                col_local(k, n).start()

            @pl.when(jnp.logical_not(here))
            def _():
                col_copy(k, n).start()

        return carry

    lax.fori_loop(0, 8, dispatch, 0)

    theirs = pl.ds(pl.multiple_of((1 - core) * 128, 128), 128)
    for n in range(2):
        fo_a[n] = (SCALE * acc_a[n, theirs, :]).astype(BF16)
    fo_b[...] = acc_v[1, theirs, :].astype(BF16)
    backs = [
        remote(fo_a, fi_a, fo_s.at[0], fo_r.at[0], at_cp(sib)),
        remote(fo_b, fi_b, fo_s.at[1], fo_r.at[1], at_cp(sib)),
    ]
    for copy in backs:
        copy.start()

    for n in (1, 3, 2):
        arrived(ypeer(n), half_a, 0)
        sib_sends.append(to_sibling(ypeer(n), half_a, 0, n))
        sib_sends[-1].start()
    arrived(xpart, half_b, 1)
    sib_sends.append(to_sibling(xpart, half_b, 1, 0))
    sib_sends[-1].start()
    for n in (1, 3, 2):
        far = (xpart + 4 * n) % 16
        arrived(far, half_a, 0)
        sib_sends.append(to_sibling(far, half_a, 0, 4 + n))
        sib_sends[-1].start()
        arrived(far, half_b, 1)
        sib_sends.append(to_sibling(far, half_b, 1, 4 + n))
        sib_sends[-1].start()

    for copy in backs:
        copy.wait()
    for n, ref in enumerate((qg_ref, kg_ref)):
        kept = (SCALE * acc_a[n, mine, :]).astype(BF16)
        got = fi_a[n]
        ref[:, 0:QK] = jnp.where(first, kept, got)
        ref[:, QK : 2 * QK] = jnp.where(first, got, kept)
    kept = acc_v[1, mine, :].astype(BF16)
    got = fi_b[...]
    vg_ref[:, 0:DH] = jnp.where(first, kept, got)
    vg_ref[:, DH : 2 * DH] = jnp.where(first, got, kept)

    remote(hid.at[sib], hid.at[sib], ho_s.at[2, 0], h_r.at[2, sib], at_cp(sib)).wait_recv()

    def from_sibling(n, carry):
        owner = (sib + 2 * n) % 16
        arrived(owner, half_a, 0)
        arrived(owner, half_b, 1)
        return carry

    lax.fori_loop(1, 8, from_sibling, 0)

    def col_wait(n, carry):
        here = (n == c) & (c // 8 == xl)

        @pl.when(here)
        def _():
            pltpu.make_async_copy(send.at[0, 0], cols.at[n], loc_s).wait()

        @pl.when(jnp.logical_not(here))
        def _():
            remote(send.at[0, 0], cols.at[n], cl_s.at[0, 0], cl_r.at[n], at_cp(sib)).wait_recv()

        return carry

    lax.fori_loop(0, 16, col_wait, 0)

    right = cols[...].reshape(16 * CAP, 448)

    def product(n, carry):
        tile = pl.ds(pl.multiple_of(n * 256, 256), 256)
        left = hid[:, :, tile].reshape(16 * CAP, 256)
        dg_ref[0, tile, :] = dot_tn(left, right).astype(BF16)
        return carry

    lax.fori_loop(0, 8, product, 0)

    for copy in swaps + own_sends + fwd_sends + sib_sends + [whole]:
        copy.wait_send()

    def att_sent(n, carry):
        for copy in att_copies(n):
            copy.wait_send()
        return carry

    lax.fori_loop(1, 8, att_sent, 0)

    def ring_sent(s, carry):
        ring_copy(True, s).wait_send()
        ring_copy(False, s).wait_send()
        return carry

    lax.fori_loop(0, 7, ring_sent, 0)
    ring_copy(True, 7).wait_send()
    ring_copy(False, 7).wait_send()

    def cols_sent(k, carry):
        for n in range(2):

            @pl.when(jnp.logical_not((col_target(k) == c) & (n == xl)))
            def _():
                col_copy(k, n).wait_send()

        return carry

    lax.fori_loop(0, 8, cols_sent, 0)


def local(*args):
    vmem = pl.BlockSpec(memory_space=pltpu.VMEM)
    dma = pltpu.SemaphoreType.DMA
    return pl.pallas_call(
        kernel,
        out_shape=(
            jax.ShapeDtypeStruct((128, 2 * QK), BF16),
            jax.ShapeDtypeStruct((128, 2 * QK), BF16),
            jax.ShapeDtypeStruct((128, 2 * DH), BF16),
            jax.ShapeDtypeStruct((1, 2048, 448), BF16),
        ),
        in_specs=[vmem] * 10,
        out_specs=(vmem,) * 4,
        scratch_shapes=[
            pltpu.VMEM((2, 256, QK), BF16),
            pltpu.VMEM((2, 256, DH), BF16),
            pltpu.VMEM((2, 8, 128), F32),
            pltpu.VMEM((2, 128, QK), BF16),
            pltpu.VMEM((2, 128, DH), BF16),
            pltpu.VMEM((8, 128), F32),
            pltpu.VMEM((8, 256, QK), BF16),
            pltpu.VMEM((8, 256, DH), BF16),
            pltpu.VMEM((8, 2, 8, 128), F32),
            pltpu.VMEM((2, 256, QK), F32),
            pltpu.VMEM((2, 256, DH), F32),
            pltpu.VMEM((2, 128, QK), BF16),
            pltpu.VMEM((128, DH), BF16),
            pltpu.VMEM((2, 128, QK), BF16),
            pltpu.VMEM((128, DH), BF16),
            pltpu.VMEM((16, 128, 224), BF16),
            pltpu.VMEM((8, 2, CAP, 448), BF16),
            pltpu.VMEM((16, CAP, 448), BF16),
            pltpu.VMEM((16, CAP, 2048), BF16),
            dma((3,)),
            dma((3,)),
            dma((3, 8)),
            dma((3, 8)),
            dma((2,)),
            dma((2,)),
            dma((2, 8)),
            dma((2, 8)),
            dma((8, 2)),
            dma((16,)),
            dma,
            dma((3, 4)),
            dma((4,)),
            dma((4,)),
            dma((2, 8)),
            dma((3, 16)),
        ],
        compiler_params=pltpu.CompilerParams(
            collective_id=0, has_side_effects=True, vmem_limit_bytes=48 * 2**20
        ),
    )(*args)


def solution(mesh):
    return jax.shard_map(
        local,
        mesh=mesh,
        in_specs=(
            P("cp", "ep"),
            P("cp", "ep"),
            P("cp", "ep"),
            P("cp", "ep"),
            P("cp", "ep"),
            P("ep", "cp"),
            P("cp", "ep"),
            P("cp", None),
            P("cp", None),
            P("ep", "cp", None),
        ),
        out_specs=(P("cp", "ep"), P("cp", "ep"), P("cp", "ep"), P("ep", None, "cp")),
        check_vma=False,
    )
```

```python
import jax
import jax.numpy as jnp
from jax import lax
from jax.experimental import pallas as pl
from jax.experimental.pallas import tpu as pltpu
from jax.sharding import PartitionSpec as P

QK = 192
DH = 128
CAP = 64
SHARE = 224
BOTH = QK + DH
SCALE = QK ** (-0.5)
MESH = pl.DeviceIdType.MESH
F32 = jnp.float32
BF16 = jnp.bfloat16


def dot_nn(a, b):
    return lax.dot_general(a, b, (((1,), (0,)), ((), ())), preferred_element_type=F32)


def dot_nt(a, b):
    return lax.dot_general(a, b, (((1,), (1,)), ((), ())), preferred_element_type=F32)


def kernel(
    q_in,
    k_in,
    v_in,
    do_in,
    o_in,
    ln_in,
    lg_in,
    gp_in,
    id_in,
    hid_in,
    qg_ref,
    kg_ref,
    vg_ref,
    dg_ref,
    q_ref,
    k_ref,
    v_ref,
    do_ref,
    o_ref,
    ln_ref,
    gp_ref,
    id_ref,
    own_t,
    own_x,
    own_y,
    own_l,
    sw_t,
    sw_l,
    far_t,
    far_l,
    acc_a,
    acc_v,
    fo_a,
    fo_b,
    fi_a,
    fi_b,
    ring,
    send,
    cols,
    left,
    hid,
    in_s,
    sw_s,
    sw_r,
    at_s,
    at_r,
    fo_s,
    fo_r,
    rg_s,
    rg_r,
    cl_s,
    cl_r,
    ho_s,
    ha_s,
    hb_s,
    hd_s,
    h_r,
):
    c = lax.axis_index("cp")
    e = lax.axis_index("ep")
    core = c % 2
    chip = c // 2
    z = e % 16
    xl = e // 16
    sib = c + 1 - 2 * core
    xpart = c + 2 - 4 * (chip % 2)
    cross = e + 16 - 32 * xl

    def at_cp(other):
        return (other, e)

    def remote(src, dst, s_sem, r_sem, target):
        return pltpu.make_async_remote_copy(
            src_ref=src,
            dst_ref=dst,
            send_sem=s_sem,
            recv_sem=r_sem,
            device_id=target,
            device_id_type=MESH,
        )

    barrier = pltpu.get_barrier_semaphore()

    def greet_cp(n, carry):
        pl.semaphore_signal(barrier, inc=1, device_id=at_cp((c + n) % 16), device_id_type=MESH)
        return carry

    lax.fori_loop(1, 16, greet_cp, 0)
    for far in (1, 2, 4, 8, 12, 14, 15):
        near = xl * 16 + (z + far) % 16
        pl.semaphore_signal(barrier, inc=1, device_id=(c, near), device_id_type=MESH)

    @pl.when(c // 8 != xl)
    def _():
        def greet_cross(n, carry):
            pl.semaphore_signal(barrier, inc=1, device_id=(n, cross), device_id_type=MESH)
            return carry

        lax.fori_loop(0, 16, greet_cross, 0)

    loads = []
    for n, (src, dst) in enumerate(
        (
            (q_in, q_ref),
            (k_in, k_ref),
            (v_in, v_ref),
            (do_in, do_ref),
            (o_in, o_ref),
            (ln_in, ln_ref),
            (lg_in, ring.at[z]),
            (gp_in, gp_ref),
            (id_in, id_ref),
            (hid_in.at[0], hid.at[c]),
        )
    ):
        copy = pltpu.make_async_copy(src, dst, in_s.at[n])
        copy.start()
        loads.append(copy)

    first = core == 0
    mine = pl.ds(pl.multiple_of(core * 128, 128), 128)
    lane = lax.broadcasted_iota(jnp.int32, (128, 128), 1)

    def stage():
        for copy in loads[0:6]:
            copy.wait()
        for side, (wide, narrow) in enumerate(((q_ref, do_ref), (k_ref, v_ref))):
            for ref, size, at in ((wide, QK, 0), (narrow, DH, QK)):
                turned = ref[...].T
                h0, h1 = turned[0:size], turned[size : 2 * size]
                own_t[side, at : at + size, mine] = jnp.where(first, h0, h1)
                sw_t[side, at : at + size, :] = jnp.where(first, h1, h0)
        prod = do_ref[...].astype(F32) * o_ref[...].astype(F32)
        d0 = jnp.sum(prod[:, 0:DH], axis=1, keepdims=True)
        d1 = jnp.sum(prod[:, DH : 2 * DH], axis=1, keepdims=True)
        rows_d = jnp.where(lane == 0, d0, jnp.where(lane == 1, d1, 0.0)).T[0:8, :]
        rows_n = ln_ref[...]
        sub = lax.broadcasted_iota(jnp.int32, (8, 128), 0)
        l0 = jnp.where(sub == 0, rows_n[0:1, :], rows_d[0:1, :])
        l1 = jnp.where(sub == 0, rows_n[1:2, :], rows_d[1:2, :])
        own_l[core] = jnp.where(first, l0, l1)
        sw_l[...] = jnp.where(first, l1, l0)

    def z_copy(group, far, n, first_hand):
        block = (z + 4 * group) % 16
        src = lg_in if first_hand else ring.at[block]
        target = xl * 16 + (z + 16 + far) % 16
        return remote(src, ring.at[block], rg_s.at[group, n], rg_r.at[block], (c, target))

    z_first = [z_copy(0, far, n, True) for n, far in enumerate((4, -4, 8, 1, -1, 2))]
    z_later = [
        [z_copy(group, far, n, False) for n, far in enumerate(fars)]
        for group, fars in ((1, (1, -1, 2, -2)), (3, (-1, 1)), (2, (1, -1, -2)))
    ]

    def z_arrived(block):
        remote(ring.at[block], ring.at[block], rg_s.at[0, 0], rg_r.at[block], at_cp(sib)).wait_recv()

    def z_pass():
        for group, copies in zip((1, 3, 2), z_later):
            z_arrived((z + 4 * group) % 16)
            start(copies)

    swaps = [
        remote(sw_t, own_t.at[:, :, mine], sw_s.at[0], sw_r.at[0], at_cp(sib)),
        remote(sw_l, own_l.at[core], sw_s.at[1], sw_r.at[1], at_cp(sib)),
    ]

    half_a, half_b = pl.ds(0, 32), pl.ds(32, 32)

    def ypeer(n):
        return (c + 4 * n) % 16

    def piece(owner, half):
        return hid.at[owner, half, :]

    def own_piece(n, target, half, col):
        return remote(
            hid_in.at[0, half, :], piece(c, half), ho_s.at[col, n], h_r.at[col, c], at_cp(target)
        )

    own_sends = [
        own_piece(n, target, half, col)
        for n, target, half, col in (
            (0, xpart, half_a, 0),
            (1, ypeer(1), half_a, 0),
            (3, ypeer(3), half_b, 1),
            (0, xpart, half_b, 1),
            (1, ypeer(1), half_b, 1),
            (3, ypeer(3), half_a, 0),
        )
    ]

    def att_copy(origin, source, rows, n, target):
        return (
            remote(source, far_t.at[origin], at_s.at[0, n], at_r.at[0, origin], at_cp(target)),
            remote(rows, far_l.at[origin], at_s.at[1, n], at_r.at[1, origin], at_cp(target)),
        )

    def att_own_copies(n, other):
        pick = jnp.where(other // 2 > chip, 1, 0)
        return att_copy(chip, own_t.at[pick], own_l, n, other)

    def att_passed(n):
        origin = (chip + 8 - 2 * n) % 8
        return att_copy(origin, far_t.at[origin], far_l.at[origin], 3 + n, xpart)

    def att_wait(origin):
        for copy in att_copy(origin, own_t.at[0], own_l, 0, sib):
            copy.wait_recv()

    def att_relay(n):
        att_wait((chip + 8 - 2 * n) % 8)
        start(att_passed(n))

    att_sends = [copy for n in (1, 3, 2) for copy in att_own_copies(n, (c + 4 * n) % 16)]
    att_sends += att_own_copies(0, xpart)
    whole = remote(hid_in.at[0], hid.at[c], ho_s.at[2, 0], h_r.at[2, c], at_cp(sib))

    def start(copies):
        for copy in copies:
            copy.start()

    def col_target(k):
        return xl * 8 + k

    def col_copy(k, n):
        return remote(
            send.at[k, n], cols.at[c], cl_s.at[k, n], cl_r.at[c], (col_target(k), n * 16 + z)
        )

    def dispatch(step, carry):
        k = (z // 2 + step + c // 4 + 2 * (c % 4)) % 8
        r0 = gate_0 * dot_nt(ring[2 * k], table_0)
        r1 = gate_1 * dot_nt(ring[2 * k + 1], table_1)
        for n, rows in enumerate((jnp.where(low, r0, r1), jnp.where(low, r1, r0))):
            send[k, n] = rows.astype(BF16)
            here = (col_target(k) == c) & (n == xl)

            @pl.when(here)
            def _():
                cols[c] = send[k, n]

            @pl.when(jnp.logical_not(here))
            def _():
                col_copy(k, n).start()

        return carry

    def dispatch_all():
        for block in range(1, 16):
            if block % 4:
                z_arrived((z + block) % 16)
        lax.fori_loop(0, 8, dispatch, 0)

    def joined(rows, n):
        return jnp.concatenate([rows[0, n : n + 1, :], rows[1, n : n + 1, :]], axis=1)

    def block(side, at, n, norm, delta, mask):
        a, b = at[n, 0:QK, :], at[n, QK:BOTH, :]
        probs = jnp.exp(SCALE * dot_nn(own_x[side], a) - norm)
        if mask is not None:
            probs = jnp.where(mask, probs, 0.0)
        ds = (probs * (dot_nn(own_y[side], b) - delta)).astype(BF16)
        return dot_nt(ds, a), dot_nt(probs.astype(BF16), b)

    def att_own():
        r_iota = lax.broadcasted_iota(jnp.int32, (256, 256), 0)
        c_iota = lax.broadcasted_iota(jnp.int32, (256, 256), 1)
        q_part, _ = block(0, own_t, 1, norm_col, delta_col, r_iota >= c_iota)
        k_part, v_part = block(1, own_t, 0, norm_row, delta_row, c_iota >= r_iota)
        acc_a[0] = q_part
        acc_a[1] = k_part
        acc_v[0] = jnp.zeros((256, DH), F32)
        acc_v[1] = v_part

    def att_step(other):
        side = jnp.where(other > chip, 1, 0)
        rows = far_l[other]
        is_far = other > chip
        norm = jnp.where(is_far, joined(rows, 0), norm_col)
        delta = jnp.where(is_far, joined(rows, 1), delta_col)
        part_a, part_v = block(side, far_t, other, norm, delta, None)
        acc_a[side] += part_a
        acc_v[side] += part_v

    def att_near(n, carry):
        att_step((chip + 8 - 2 * n) % 8)
        return carry

    def att_far(n, carry):
        other = (xpart // 2 + 8 - 2 * n) % 8
        att_wait(other)
        att_step(other)
        return carry

    sib_sends = []
    fwd_sends = []

    def arrived(owner, half, col):
        remote(
            piece(owner, half), piece(owner, half), hd_s.at[col, 0], h_r.at[col, owner], at_cp(sib)
        ).wait_recv()

    def to_sibling(owner, half, col, n):
        copy = remote(
            piece(owner, half), piece(owner, half), hd_s.at[col, n], h_r.at[col, owner], at_cp(sib)
        )
        copy.start()
        sib_sends.append(copy)

    def forward(owner, half, col, sem, target):
        copy = remote(piece(owner, half), piece(owner, half), sem, h_r.at[col, owner], at_cp(target))
        copy.start()
        fwd_sends.append(copy)

    def far_peer(n):
        return (xpart + 4 * n) % 16

    def relay_x(half, col):
        arrived(xpart, half, col)
        for n in (1, 3):
            forward(xpart, half, col, hb_s.at[2 * col + n // 2], ypeer(n))
        to_sibling(xpart, half, col, 0)

    def relay_y(n, near):
        owner = ypeer(n) if near else far_peer(n)
        half, col = (half_a, 0) if n == 3 else (half_b, 1)
        arrived(owner, half, col)
        forward(owner, half, col, ha_s.at[2 * near + col], ypeer(4 - n))
        to_sibling(owner, half, col, n + 4 * (1 - near))

    def keep_y(n, near, half, col):
        owner = ypeer(n) if near else far_peer(n)
        arrived(owner, half, col)
        to_sibling(owner, half, col, n + 4 * (1 - near))

    pl.semaphore_wait(barrier, 30)
    start(z_first)
    start(own_sends)
    stage()
    start(swaps)

    for copy in loads[6:]:
        copy.wait()
    ids = id_ref[...]
    gates = gp_ref[...]
    before_t = (lax.broadcasted_iota(jnp.int32, (128, 128), 0) < lane).astype(BF16)
    spots = lax.broadcasted_iota(jnp.int32, (CAP, 128), 0).astype(F32)
    tables, weights = [], []
    for n in range(2):
        hit = ids == 16 * n + z
        named = jnp.sum(jnp.where(hit, 1.0, 0.0), axis=0, keepdims=True)
        gate = jnp.sum(jnp.where(hit, gates, 0.0), axis=0, keepdims=True)
        earlier = dot_nn(jnp.broadcast_to(named, (8, 128)).astype(BF16), before_t)[0:1, :]
        inside = (spots == earlier) & (named > 0.5)
        tables.append(jnp.where(inside, 1.0, 0.0))
        weights.append(jnp.where(inside, gate, 0.0))
    table_0 = jnp.concatenate(tables, axis=0).astype(BF16)
    table_1 = jnp.concatenate(tables[::-1], axis=0).astype(BF16)
    gate_0 = jnp.sum(jnp.concatenate(weights, axis=0).T, axis=0, keepdims=True)
    gate_1 = jnp.sum(jnp.concatenate(weights[::-1], axis=0).T, axis=0, keepdims=True)
    low = lax.broadcasted_iota(jnp.int32, (SHARE, 128), 1) < CAP

    for copy in swaps:
        copy.wait_recv()
    start(att_sends)
    start([whole])
    relay_x(half_a, 0)
    relay_x(half_b, 1)
    relay_y(3, 1)
    relay_y(1, 1)
    att_relay(1)
    att_relay(3)
    z_pass()
    att_relay(2)
    relay_y(3, 0)
    relay_y(1, 0)
    for side in range(2):
        own_x[side] = own_t[side, 0:QK, :].T
        own_y[side] = own_t[side, QK:BOTH, :].T

    own_rows = own_l[...]
    norm_row, delta_row = joined(own_rows, 0), joined(own_rows, 1)
    turned_l = [
        jnp.concatenate([own_rows[n], jnp.zeros((120, 128), F32)], axis=0).T for n in range(2)
    ]
    norm_col = jnp.concatenate([turned_l[0][:, 0:1], turned_l[1][:, 0:1]], axis=0)
    delta_col = jnp.concatenate([turned_l[0][:, 1:2], turned_l[1][:, 1:2]], axis=0)
    att_own()
    lax.fori_loop(1, 4, att_near, 0)
    dispatch_all()
    lax.fori_loop(0, 4, att_far, 0)
    theirs = pl.ds(pl.multiple_of((1 - core) * 128, 128), 128)
    for n in range(2):
        fo_a[n] = (SCALE * acc_a[n, theirs, :]).astype(BF16)
    fo_b[...] = acc_v[1, theirs, :].astype(BF16)
    backs = [
        remote(fo_a, fi_a, fo_s.at[0], fo_r.at[0], at_cp(sib)),
        remote(fo_b, fi_b, fo_s.at[1], fo_r.at[1], at_cp(sib)),
    ]
    for copy in backs:
        copy.start()
    for near in (1, 0):
        keep_y(1, near, half_a, 0)
        keep_y(3, near, half_b, 1)
        keep_y(2, near, half_a, 0)
        keep_y(2, near, half_b, 1)

    for copy in backs:
        copy.wait()
    for n, ref in enumerate((qg_ref, kg_ref)):
        kept = (SCALE * acc_a[n, mine, :]).astype(BF16)
        got = fi_a[n]
        ref[:, 0:QK] = jnp.where(first, kept, got)
        ref[:, QK : 2 * QK] = jnp.where(first, got, kept)
    kept = acc_v[1, mine, :].astype(BF16)
    got = fi_b[...]
    vg_ref[:, 0:DH] = jnp.where(first, kept, got)
    vg_ref[:, DH : 2 * DH] = jnp.where(first, got, kept)

    remote(hid.at[sib], hid.at[sib], ho_s.at[2, 0], h_r.at[2, sib], at_cp(sib)).wait_recv()

    def from_sibling(n, carry):
        owner = (sib + 2 * n) % 16
        arrived(owner, half_a, 0)
        arrived(owner, half_b, 1)
        return carry

    lax.fori_loop(1, 8, from_sibling, 0)

    def col_wait(n, carry):
        @pl.when(jnp.logical_not((n == c) & (c // 8 == xl)))
        def _():
            remote(send.at[0, 0], cols.at[n], cl_s.at[0, 0], cl_r.at[n], at_cp(sib)).wait_recv()

        return carry

    lax.fori_loop(0, 16, col_wait, 0)

    for m in range(8):
        p0, p1 = cols[2 * m], cols[2 * m + 1]
        t0 = jnp.concatenate([p0[:, 0:CAP], p1[:, 0:CAP]], axis=1)
        t1 = jnp.concatenate([p0[:, CAP : 2 * CAP], p1[:, CAP : 2 * CAP]], axis=1)
        left[0:SHARE, 128 * m : 128 * m + 128] = jnp.where(xl == 0, t0, t1)
        left[SHARE : 2 * SHARE, 128 * m : 128 * m + 128] = jnp.where(xl == 0, t1, t0)

    def product(n, carry):
        tile = pl.ds(pl.multiple_of(n * 256, 256), 256)
        right = hid[:, :, tile].reshape(16 * CAP, 256)
        dg_ref[0, :, tile] = dot_nn(left[...], right).astype(BF16)
        return carry

    lax.fori_loop(0, 8, product, 0)

    for copy in swaps + own_sends + fwd_sends + sib_sends + [whole] + att_sends + z_first + sum(z_later, []):
        copy.wait_send()

    for n in (1, 2, 3):
        for copy in att_passed(n):
            copy.wait_send()

    def cols_sent(k, carry):
        for n in range(2):

            @pl.when(jnp.logical_not((col_target(k) == c) & (n == xl)))
            def _():
                col_copy(k, n).wait_send()

        return carry

    lax.fori_loop(0, 8, cols_sent, 0)


def put_out(*refs):
    ins, outs, sems = refs[0:4], refs[4:8], refs[8]
    copies = [pltpu.make_async_copy(a, b, sems.at[n]) for n, (a, b) in enumerate(zip(ins, outs))]
    for copy in copies:
        copy.start()
    for copy in copies:
        copy.wait()


def local(q, k, v, do, o, ln, lg, gp, ids, hidden):
    vmem = pl.BlockSpec(memory_space=pltpu.VMEM)
    hbm = pl.BlockSpec(memory_space=pltpu.HBM)
    dma = pltpu.SemaphoreType.DMA
    shapes = (
        jax.ShapeDtypeStruct((128, 2 * QK), BF16),
        jax.ShapeDtypeStruct((128, 2 * QK), BF16),
        jax.ShapeDtypeStruct((128, 2 * DH), BF16),
        jax.ShapeDtypeStruct((1, 2 * SHARE, 2048), BF16),
    )
    results = pl.pallas_call(
        kernel,
        out_shape=shapes,
        in_specs=[hbm] * 10,
        out_specs=(vmem,) * 4,
        scratch_shapes=[
            pltpu.VMEM((128, 2 * QK), BF16),
            pltpu.VMEM((128, 2 * QK), BF16),
            pltpu.VMEM((128, 2 * DH), BF16),
            pltpu.VMEM((128, 2 * DH), BF16),
            pltpu.VMEM((128, 2 * DH), BF16),
            pltpu.VMEM((2, 128), F32),
            pltpu.VMEM((8, 128), F32),
            pltpu.VMEM((8, 128), jnp.int32),
            pltpu.VMEM((2, BOTH, 256), BF16),
            pltpu.VMEM((2, 256, QK), BF16),
            pltpu.VMEM((2, 256, DH), BF16),
            pltpu.VMEM((2, 8, 128), F32),
            pltpu.VMEM((2, BOTH, 128), BF16),
            pltpu.VMEM((8, 128), F32),
            pltpu.VMEM((8, BOTH, 256), BF16),
            pltpu.VMEM((8, 2, 8, 128), F32),
            pltpu.VMEM((2, 256, QK), F32),
            pltpu.VMEM((2, 256, DH), F32),
            pltpu.VMEM((2, 128, QK), BF16),
            pltpu.VMEM((128, DH), BF16),
            pltpu.VMEM((2, 128, QK), BF16),
            pltpu.VMEM((128, DH), BF16),
            pltpu.VMEM((16, SHARE, 128), BF16),
            pltpu.VMEM((8, 2, SHARE, 128), BF16),
            pltpu.VMEM((16, SHARE, 128), BF16),
            pltpu.VMEM((2 * SHARE, 16 * CAP), BF16),
            pltpu.VMEM((16, CAP, 2048), BF16),
            dma((10,)),
            dma((2,)),
            dma((2,)),
            dma((2, 8)),
            dma((2, 8)),
            dma((2,)),
            dma((2,)),
            dma((4, 6)),
            dma((16,)),
            dma((8, 2)),
            dma((16,)),
            dma((3, 4)),
            dma((4,)),
            dma((4,)),
            dma((2, 8)),
            dma((3, 16)),
        ],
        compiler_params=pltpu.CompilerParams(
            collective_id=0, has_side_effects=True, vmem_limit_bytes=60 * 2**20
        ),
    )(q, k, v, do, o, ln, lg.T, gp.T, ids.T, hidden)
    q_grad, k_grad, v_grad, down = pl.pallas_call(
        put_out,
        out_shape=shapes,
        in_specs=[vmem] * 4,
        out_specs=(hbm,) * 4,
        scratch_shapes=[dma((4,))],
    )(*results)
    return q_grad, k_grad, v_grad, jnp.swapaxes(down, 1, 2)


def solution(mesh):
    return jax.shard_map(
        local,
        mesh=mesh,
        in_specs=(
            P("cp", "ep"),
            P("cp", "ep"),
            P("cp", "ep"),
            P("cp", "ep"),
            P("cp", "ep"),
            P("ep", "cp"),
            P("cp", "ep"),
            P("cp", None),
            P("cp", None),
            P("ep", "cp", None),
        ),
        out_specs=(P("cp", "ep"), P("cp", "ep"), P("cp", "ep"), P("ep", None, "cp")),
        check_vma=False,
    )
```

```python
import jax
import jax.numpy as jnp
from jax import lax
from jax.experimental import pallas as pl
from jax.experimental.pallas import tpu as pltpu
from jax.sharding import PartitionSpec as P

QK = 192
DH = 128
CAP = 64
SHARE = 224
BOTH = QK + DH
SCALE = QK ** (-0.5)
MESH = pl.DeviceIdType.MESH
F32 = jnp.float32
BF16 = jnp.bfloat16


def dot_nn(a, b):
    return lax.dot_general(a, b, (((1,), (0,)), ((), ())), preferred_element_type=F32)


def dot_nt(a, b):
    return lax.dot_general(a, b, (((1,), (1,)), ((), ())), preferred_element_type=F32)


def kernel(
    q_in,
    k_in,
    v_in,
    do_in,
    o_in,
    ln_in,
    lg_in,
    gp_in,
    id_in,
    hid_in,
    qg_ref,
    kg_ref,
    vg_ref,
    dg_ref,
    q_ref,
    k_ref,
    v_ref,
    do_ref,
    o_ref,
    ln_ref,
    gp_ref,
    id_ref,
    own_t,
    own_x,
    own_y,
    own_l,
    sw_t,
    sw_l,
    far_t,
    far_l,
    acc_a,
    acc_v,
    fo_a,
    fo_b,
    fi_a,
    fi_b,
    ring,
    send,
    cols,
    left,
    hid,
    in_s,
    sw_s,
    sw_r,
    at_s,
    at_r,
    fo_s,
    fo_r,
    rg_s,
    rg_r,
    cl_s,
    cl_r,
    ho_s,
    ha_s,
    hb_s,
    hd_s,
    h_r,
):
    c = lax.axis_index("cp")
    e = lax.axis_index("ep")
    core = c % 2
    chip = c // 2
    z = e % 16
    xl = e // 16
    sib = c + 1 - 2 * core
    xpart = c + 2 - 4 * (chip % 2)
    cross = e + 16 - 32 * xl

    def at_cp(other):
        return (other, e)

    def remote(src, dst, s_sem, r_sem, target):
        return pltpu.make_async_remote_copy(
            src_ref=src,
            dst_ref=dst,
            send_sem=s_sem,
            recv_sem=r_sem,
            device_id=target,
            device_id_type=MESH,
        )

    barrier = pltpu.get_barrier_semaphore()

    def greet_cp(n, carry):
        pl.semaphore_signal(barrier, inc=1, device_id=at_cp((c + n) % 16), device_id_type=MESH)
        return carry

    lax.fori_loop(1, 16, greet_cp, 0)
    for far in (1, 2, 3, 13, 14, 15):
        near = xl * 16 + (z + far) % 16
        pl.semaphore_signal(barrier, inc=1, device_id=(c, near), device_id_type=MESH)

    @pl.when(c // 8 != xl)
    def _():
        def greet_cross(n, carry):
            pl.semaphore_signal(barrier, inc=1, device_id=(n, cross), device_id_type=MESH)
            return carry

        lax.fori_loop(0, 16, greet_cross, 0)

    loads = []
    for n, (src, dst) in enumerate(
        (
            (q_in, q_ref),
            (k_in, k_ref),
            (v_in, v_ref),
            (do_in, do_ref),
            (o_in, o_ref),
            (ln_in, ln_ref),
            (lg_in, ring.at[z]),
            (gp_in, gp_ref),
            (id_in, id_ref),
            (hid_in.at[0], hid.at[c]),
        )
    ):
        copy = pltpu.make_async_copy(src, dst, in_s.at[n])
        copy.start()
        loads.append(copy)

    first = core == 0
    mine = pl.ds(pl.multiple_of(core * 128, 128), 128)
    lane = lax.broadcasted_iota(jnp.int32, (128, 128), 1)

    def stage():
        for copy in loads[0:6]:
            copy.wait()
        for side, (wide, narrow) in enumerate(((q_ref, do_ref), (k_ref, v_ref))):
            for ref, size, at in ((wide, QK, 0), (narrow, DH, QK)):
                turned = ref[...].T
                h0, h1 = turned[0:size], turned[size : 2 * size]
                own_t[side, at : at + size, mine] = jnp.where(first, h0, h1)
                sw_t[side, at : at + size, :] = jnp.where(first, h1, h0)
        prod = do_ref[...].astype(F32) * o_ref[...].astype(F32)
        d0 = jnp.sum(prod[:, 0:DH], axis=1, keepdims=True)
        d1 = jnp.sum(prod[:, DH : 2 * DH], axis=1, keepdims=True)
        rows_d = jnp.where(lane == 0, d0, jnp.where(lane == 1, d1, 0.0)).T[0:8, :]
        rows_n = ln_ref[...]
        sub = lax.broadcasted_iota(jnp.int32, (8, 128), 0)
        l0 = jnp.where(sub == 0, rows_n[0:1, :], rows_d[0:1, :])
        l1 = jnp.where(sub == 0, rows_n[1:2, :], rows_d[1:2, :])
        own_l[core] = jnp.where(first, l0, l1)
        sw_l[...] = jnp.where(first, l1, l0)

    def z_copy(back, far, n, rows, sem):
        block = (z + 16 + back) % 16
        ref = ring.at[block, rows, :]
        src = lg_in if back == 0 else ref
        target = xl * 16 + (z + 16 + far) % 16
        return remote(src, ref, rg_s.at[n], rg_r.at[block if sem is None else sem], (c, target))

    z_all = pl.ds(0, SHARE)
    z_half = (pl.ds(0, SHARE // 2), pl.ds(SHARE // 2, SHARE // 2))
    z_first = [z_copy(0, far, n, z_all, None) for n, far in enumerate((3, -3, 1, -1))]
    z_later = [
        [z_copy(-3, far, 4 + n, z_all, None) for n, far in enumerate((3, 1, -1))],
        [z_copy(3, far, 7 + n, z_all, None) for n, far in enumerate((-3, -1, 1))],
        [z_copy(-6, far, 10 + n, z_all, None) for n, far in enumerate((1, -1))]
        + [z_copy(-6, 2, 12, z_half[0], None)],
        [z_copy(6, far, 13 + n, z_all, None) for n, far in enumerate((-1, 1))]
        + [z_copy(6, -2, 15, z_half[1], 16)],
    ]

    def z_arrived(block, rows, sem):
        ref = ring.at[block, rows, :]
        remote(ref, ref, rg_s.at[0], rg_r.at[sem], at_cp(sib)).wait_recv()

    def z_pass(n):
        block = (z + (13, 3, 10, 6)[n]) % 16
        z_arrived(block, z_all, block)
        start(z_later[n])

    swaps = [
        remote(sw_t, own_t.at[:, :, mine], sw_s.at[0], sw_r.at[0], at_cp(sib)),
        remote(sw_l, own_l.at[core], sw_s.at[1], sw_r.at[1], at_cp(sib)),
    ]

    half_a, half_b = pl.ds(0, 32), pl.ds(32, 32)

    def ypeer(n):
        return (c + 4 * n) % 16

    def piece(owner, half):
        return hid.at[owner, half, :]

    def own_piece(n, target, half, col):
        return remote(
            hid_in.at[0, half, :], piece(c, half), ho_s.at[col, n], h_r.at[col, c], at_cp(target)
        )

    own_sends = [
        own_piece(n, target, half, col)
        for n, target, half, col in (
            (0, xpart, half_a, 0),
            (1, ypeer(1), half_a, 0),
            (3, ypeer(3), half_b, 1),
            (0, xpart, half_b, 1),
            (1, ypeer(1), half_b, 1),
            (3, ypeer(3), half_a, 0),
        )
    ]

    def att_copy(origin, source, rows, n, target):
        return (
            remote(source, far_t.at[origin], at_s.at[0, n], at_r.at[0, origin], at_cp(target)),
            remote(rows, far_l.at[origin], at_s.at[1, n], at_r.at[1, origin], at_cp(target)),
        )

    def att_own_copies(n, other):
        pick = jnp.where(other // 2 > chip, 1, 0)
        return att_copy(chip, own_t.at[pick], own_l, n, other)

    def att_passed(n):
        origin = (chip + 8 - 2 * n) % 8
        return att_copy(origin, far_t.at[origin], far_l.at[origin], 3 + n, xpart)

    def att_wait(origin):
        for copy in att_copy(origin, own_t.at[0], own_l, 0, sib):
            copy.wait_recv()

    def att_relay(n):
        att_wait((chip + 8 - 2 * n) % 8)
        start(att_passed(n))

    att_sends = [copy for n in (1, 3, 2) for copy in att_own_copies(n, (c + 4 * n) % 16)]
    att_sends += att_own_copies(0, xpart)
    whole = remote(hid_in.at[0], hid.at[c], ho_s.at[2, 0], h_r.at[2, c], at_cp(sib))

    def start(copies):
        for copy in copies:
            copy.start()

    def col_target(k):
        return xl * 8 + k

    def col_copy(k, n):
        return remote(
            send.at[k, n], cols.at[c], cl_s.at[k, n], cl_r.at[c], (col_target(k), n * 16 + z)
        )

    def dispatch(step, carry):
        k = (z // 2 + step + c // 4 + 2 * (c % 4)) % 8
        r0 = gate_0 * dot_nt(ring[2 * k], table_0)
        r1 = gate_1 * dot_nt(ring[2 * k + 1], table_1)
        for n, rows in enumerate((jnp.where(low, r0, r1), jnp.where(low, r1, r0))):
            send[k, n] = rows.astype(BF16)
            here = (col_target(k) == c) & (n == xl)

            @pl.when(here)
            def _():
                cols[c] = send[k, n]

            @pl.when(jnp.logical_not(here))
            def _():
                col_copy(k, n).start()

        return carry

    def dispatch_all():
        for far in (1, 15, 2, 14, 4, 12, 5, 11, 7, 9):
            z_arrived((z + far) % 16, z_all, (z + far) % 16)
        opposite = (z + 8) % 16
        z_arrived(opposite, z_half[0], opposite)
        z_arrived(opposite, z_half[1], 16)
        lax.fori_loop(0, 8, dispatch, 0)

    def joined(rows, n):
        return jnp.concatenate([rows[0, n : n + 1, :], rows[1, n : n + 1, :]], axis=1)

    def block(side, at, n, norm, delta, mask):
        a, b = at[n, 0:QK, :], at[n, QK:BOTH, :]
        probs = jnp.exp(SCALE * dot_nn(own_x[side], a) - norm)
        if mask is not None:
            probs = jnp.where(mask, probs, 0.0)
        ds = (probs * (dot_nn(own_y[side], b) - delta)).astype(BF16)
        return dot_nt(ds, a), dot_nt(probs.astype(BF16), b)

    def att_own():
        r_iota = lax.broadcasted_iota(jnp.int32, (256, 256), 0)
        c_iota = lax.broadcasted_iota(jnp.int32, (256, 256), 1)
        q_part, _ = block(0, own_t, 1, norm_col, delta_col, r_iota >= c_iota)
        k_part, v_part = block(1, own_t, 0, norm_row, delta_row, c_iota >= r_iota)
        acc_a[0] = q_part
        acc_a[1] = k_part
        acc_v[0] = jnp.zeros((256, DH), F32)
        acc_v[1] = v_part

    def att_step(other):
        side = jnp.where(other > chip, 1, 0)
        rows = far_l[other]
        is_far = other > chip
        norm = jnp.where(is_far, joined(rows, 0), norm_col)
        delta = jnp.where(is_far, joined(rows, 1), delta_col)
        part_a, part_v = block(side, far_t, other, norm, delta, None)
        acc_a[side] += part_a
        acc_v[side] += part_v

    def att_near(n, carry):
        att_step((chip + 8 - 2 * n) % 8)
        return carry

    def att_far(n, carry):
        other = (xpart // 2 + 8 - 2 * n) % 8
        att_wait(other)
        att_step(other)
        return carry

    sib_sends = []
    fwd_sends = []

    def arrived(owner, half, col):
        remote(
            piece(owner, half), piece(owner, half), hd_s.at[col, 0], h_r.at[col, owner], at_cp(sib)
        ).wait_recv()

    def to_sibling(owner, half, col, n):
        copy = remote(
            piece(owner, half), piece(owner, half), hd_s.at[col, n], h_r.at[col, owner], at_cp(sib)
        )
        copy.start()
        sib_sends.append(copy)

    def forward(owner, half, col, sem, target):
        copy = remote(piece(owner, half), piece(owner, half), sem, h_r.at[col, owner], at_cp(target))
        copy.start()
        fwd_sends.append(copy)

    def far_peer(n):
        return (xpart + 4 * n) % 16

    def relay_x(half, col):
        arrived(xpart, half, col)
        for n in (1, 3):
            forward(xpart, half, col, hb_s.at[2 * col + n // 2], ypeer(n))
        to_sibling(xpart, half, col, 0)

    def relay_y(n, near):
        owner = ypeer(n) if near else far_peer(n)
        half, col = (half_a, 0) if n == 3 else (half_b, 1)
        arrived(owner, half, col)
        forward(owner, half, col, ha_s.at[2 * near + col], ypeer(4 - n))
        to_sibling(owner, half, col, n + 4 * (1 - near))

    def keep_y(n, near, half, col):
        owner = ypeer(n) if near else far_peer(n)
        arrived(owner, half, col)
        to_sibling(owner, half, col, n + 4 * (1 - near))

    pl.semaphore_wait(barrier, 29)
    start(z_first)
    start(own_sends)
    stage()
    start(swaps)

    for copy in loads[6:]:
        copy.wait()
    ids = id_ref[...]
    gates = gp_ref[...]
    before_t = (lax.broadcasted_iota(jnp.int32, (128, 128), 0) < lane).astype(BF16)
    spots = lax.broadcasted_iota(jnp.int32, (CAP, 128), 0).astype(F32)
    tables, weights = [], []
    for n in range(2):
        hit = ids == 16 * n + z
        named = jnp.sum(jnp.where(hit, 1.0, 0.0), axis=0, keepdims=True)
        gate = jnp.sum(jnp.where(hit, gates, 0.0), axis=0, keepdims=True)
        earlier = dot_nn(jnp.broadcast_to(named, (8, 128)).astype(BF16), before_t)[0:1, :]
        inside = (spots == earlier) & (named > 0.5)
        tables.append(jnp.where(inside, 1.0, 0.0))
        weights.append(jnp.where(inside, gate, 0.0))
    table_0 = jnp.concatenate(tables, axis=0).astype(BF16)
    table_1 = jnp.concatenate(tables[::-1], axis=0).astype(BF16)
    gate_0 = jnp.sum(jnp.concatenate(weights, axis=0).T, axis=0, keepdims=True)
    gate_1 = jnp.sum(jnp.concatenate(weights[::-1], axis=0).T, axis=0, keepdims=True)
    low = lax.broadcasted_iota(jnp.int32, (SHARE, 128), 1) < CAP

    for copy in swaps:
        copy.wait_recv()
    start(att_sends)
    start([whole])
    z_pass(0)
    z_pass(1)
    relay_x(half_a, 0)
    relay_x(half_b, 1)
    relay_y(3, 1)
    z_pass(2)
    z_pass(3)
    relay_y(1, 1)
    att_relay(1)
    att_relay(3)
    att_relay(2)
    relay_y(3, 0)
    relay_y(1, 0)
    for side in range(2):
        own_x[side] = own_t[side, 0:QK, :].T
        own_y[side] = own_t[side, QK:BOTH, :].T

    own_rows = own_l[...]
    norm_row, delta_row = joined(own_rows, 0), joined(own_rows, 1)
    turned_l = [
        jnp.concatenate([own_rows[n], jnp.zeros((120, 128), F32)], axis=0).T for n in range(2)
    ]
    norm_col = jnp.concatenate([turned_l[0][:, 0:1], turned_l[1][:, 0:1]], axis=0)
    delta_col = jnp.concatenate([turned_l[0][:, 1:2], turned_l[1][:, 1:2]], axis=0)
    att_own()
    lax.fori_loop(1, 4, att_near, 0)
    dispatch_all()
    lax.fori_loop(0, 4, att_far, 0)
    theirs = pl.ds(pl.multiple_of((1 - core) * 128, 128), 128)
    for n in range(2):
        fo_a[n] = (SCALE * acc_a[n, theirs, :]).astype(BF16)
    fo_b[...] = acc_v[1, theirs, :].astype(BF16)
    backs = [
        remote(fo_a, fi_a, fo_s.at[0], fo_r.at[0], at_cp(sib)),
        remote(fo_b, fi_b, fo_s.at[1], fo_r.at[1], at_cp(sib)),
    ]
    for copy in backs:
        copy.start()
    for near in (1, 0):
        keep_y(1, near, half_a, 0)
        keep_y(3, near, half_b, 1)
        keep_y(2, near, half_a, 0)
        keep_y(2, near, half_b, 1)

    for copy in backs:
        copy.wait()
    for n, ref in enumerate((qg_ref, kg_ref)):
        kept = (SCALE * acc_a[n, mine, :]).astype(BF16)
        got = fi_a[n]
        ref[:, 0:QK] = jnp.where(first, kept, got)
        ref[:, QK : 2 * QK] = jnp.where(first, got, kept)
    kept = acc_v[1, mine, :].astype(BF16)
    got = fi_b[...]
    vg_ref[:, 0:DH] = jnp.where(first, kept, got)
    vg_ref[:, DH : 2 * DH] = jnp.where(first, got, kept)

    remote(hid.at[sib], hid.at[sib], ho_s.at[2, 0], h_r.at[2, sib], at_cp(sib)).wait_recv()

    def from_sibling(n, carry):
        owner = (sib + 2 * n) % 16
        arrived(owner, half_a, 0)
        arrived(owner, half_b, 1)
        return carry

    lax.fori_loop(1, 8, from_sibling, 0)

    def col_wait(n, carry):
        @pl.when(jnp.logical_not((n == c) & (c // 8 == xl)))
        def _():
            remote(send.at[0, 0], cols.at[n], cl_s.at[0, 0], cl_r.at[n], at_cp(sib)).wait_recv()

        return carry

    lax.fori_loop(0, 16, col_wait, 0)

    for m in range(8):
        p0, p1 = cols[2 * m], cols[2 * m + 1]
        t0 = jnp.concatenate([p0[:, 0:CAP], p1[:, 0:CAP]], axis=1)
        t1 = jnp.concatenate([p0[:, CAP : 2 * CAP], p1[:, CAP : 2 * CAP]], axis=1)
        left[0:SHARE, 128 * m : 128 * m + 128] = jnp.where(xl == 0, t0, t1)
        left[SHARE : 2 * SHARE, 128 * m : 128 * m + 128] = jnp.where(xl == 0, t1, t0)

    def product(n, carry):
        tile = pl.ds(pl.multiple_of(n * 512, 512), 512)
        right = hid[:, :, tile].reshape(16 * CAP, 512)
        dg_ref[0, :, tile] = dot_nn(left[...], right).astype(BF16)
        return carry

    lax.fori_loop(0, 4, product, 0)

    for copy in swaps + own_sends + fwd_sends + sib_sends + [whole] + att_sends + z_first + sum(z_later, []):
        copy.wait_send()

    for n in (1, 2, 3):
        for copy in att_passed(n):
            copy.wait_send()

    def cols_sent(k, carry):
        for n in range(2):

            @pl.when(jnp.logical_not((col_target(k) == c) & (n == xl)))
            def _():
                col_copy(k, n).wait_send()

        return carry

    lax.fori_loop(0, 8, cols_sent, 0)


def put_out(*refs):
    ins, outs, sems = refs[0:4], refs[4:8], refs[8]
    copies = [pltpu.make_async_copy(a, b, sems.at[n]) for n, (a, b) in enumerate(zip(ins, outs))]
    for copy in copies:
        copy.start()
    for copy in copies:
        copy.wait()


def local(q, k, v, do, o, ln, lg, gp, ids, hidden):
    vmem = pl.BlockSpec(memory_space=pltpu.VMEM)
    hbm = pl.BlockSpec(memory_space=pltpu.HBM)
    dma = pltpu.SemaphoreType.DMA
    shapes = (
        jax.ShapeDtypeStruct((128, 2 * QK), BF16),
        jax.ShapeDtypeStruct((128, 2 * QK), BF16),
        jax.ShapeDtypeStruct((128, 2 * DH), BF16),
        jax.ShapeDtypeStruct((1, 2 * SHARE, 2048), BF16),
    )
    results = pl.pallas_call(
        kernel,
        out_shape=shapes,
        in_specs=[hbm] * 10,
        out_specs=(vmem,) * 4,
        scratch_shapes=[
            pltpu.VMEM((128, 2 * QK), BF16),
            pltpu.VMEM((128, 2 * QK), BF16),
            pltpu.VMEM((128, 2 * DH), BF16),
            pltpu.VMEM((128, 2 * DH), BF16),
            pltpu.VMEM((128, 2 * DH), BF16),
            pltpu.VMEM((2, 128), F32),
            pltpu.VMEM((8, 128), F32),
            pltpu.VMEM((8, 128), jnp.int32),
            pltpu.VMEM((2, BOTH, 256), BF16),
            pltpu.VMEM((2, 256, QK), BF16),
            pltpu.VMEM((2, 256, DH), BF16),
            pltpu.VMEM((2, 8, 128), F32),
            pltpu.VMEM((2, BOTH, 128), BF16),
            pltpu.VMEM((8, 128), F32),
            pltpu.VMEM((8, BOTH, 256), BF16),
            pltpu.VMEM((8, 2, 8, 128), F32),
            pltpu.VMEM((2, 256, QK), F32),
            pltpu.VMEM((2, 256, DH), F32),
            pltpu.VMEM((2, 128, QK), BF16),
            pltpu.VMEM((128, DH), BF16),
            pltpu.VMEM((2, 128, QK), BF16),
            pltpu.VMEM((128, DH), BF16),
            pltpu.VMEM((16, SHARE, 128), BF16),
            pltpu.VMEM((8, 2, SHARE, 128), BF16),
            pltpu.VMEM((16, SHARE, 128), BF16),
            pltpu.VMEM((2 * SHARE, 16 * CAP), BF16),
            pltpu.VMEM((16, CAP, 2048), BF16),
            dma((10,)),
            dma((2,)),
            dma((2,)),
            dma((2, 8)),
            dma((2, 8)),
            dma((2,)),
            dma((2,)),
            dma((16,)),
            dma((17,)),
            dma((8, 2)),
            dma((16,)),
            dma((3, 4)),
            dma((4,)),
            dma((4,)),
            dma((2, 8)),
            dma((3, 16)),
        ],
        compiler_params=pltpu.CompilerParams(
            collective_id=0, has_side_effects=True, vmem_limit_bytes=60 * 2**20
        ),
    )(q, k, v, do, o, ln, lg.T, gp.T, ids.T, hidden)
    q_grad, k_grad, v_grad, down = pl.pallas_call(
        put_out,
        out_shape=shapes,
        in_specs=[vmem] * 4,
        out_specs=(hbm,) * 4,
        scratch_shapes=[dma((4,))],
    )(*results)
    return q_grad, k_grad, v_grad, jnp.swapaxes(down, 1, 2)


def solution(mesh):
    return jax.shard_map(
        local,
        mesh=mesh,
        in_specs=(
            P("cp", "ep"),
            P("cp", "ep"),
            P("cp", "ep"),
            P("cp", "ep"),
            P("cp", "ep"),
            P("ep", "cp"),
            P("cp", "ep"),
            P("cp", None),
            P("cp", None),
            P("ep", "cp", None),
        ),
        out_specs=(P("cp", "ep"), P("cp", "ep"), P("cp", "ep"), P("ep", None, "cp")),
        check_vma=False,
    )
```

```python
import jax
import jax.numpy as jnp
from jax import lax
from jax.experimental import pallas as pl
from jax.experimental.pallas import tpu as pltpu
from jax.sharding import PartitionSpec as P

QK = 192
DH = 128
CAP = 64
SHARE = 224
BOTH = QK + DH
SCALE = QK ** (-0.5)
MESH = pl.DeviceIdType.MESH
F32 = jnp.float32
BF16 = jnp.bfloat16


def dot_nn(a, b):
    return lax.dot_general(a, b, (((1,), (0,)), ((), ())), preferred_element_type=F32)


def dot_nt(a, b):
    return lax.dot_general(a, b, (((1,), (1,)), ((), ())), preferred_element_type=F32)


def kernel(
    q_in,
    k_in,
    v_in,
    do_in,
    o_in,
    ln_in,
    lg_in,
    gp_in,
    id_in,
    hid_in,
    qg_ref,
    kg_ref,
    vg_ref,
    left,
    hid,
    q_ref,
    k_ref,
    v_ref,
    do_ref,
    o_ref,
    ln_ref,
    gp_ref,
    id_ref,
    own_t,
    own_x,
    own_y,
    own_l,
    sw_t,
    sw_l,
    far_t,
    far_l,
    acc_a,
    acc_v,
    fo_a,
    fo_b,
    fi_a,
    fi_b,
    ring,
    send,
    cols,
    in_s,
    sw_s,
    sw_r,
    at_s,
    at_r,
    fo_s,
    fo_r,
    rg_s,
    rg_r,
    cl_s,
    cl_r,
    ho_s,
    ha_s,
    hb_s,
    hd_s,
    h_r,
):
    c = lax.axis_index("cp")
    e = lax.axis_index("ep")
    core = c % 2
    chip = c // 2
    z = e % 16
    xl = e // 16
    sib = c + 1 - 2 * core
    xpart = c + 2 - 4 * (chip % 2)
    cross = e + 16 - 32 * xl

    def at_cp(other):
        return (other, e)

    def remote(src, dst, s_sem, r_sem, target):
        return pltpu.make_async_remote_copy(
            src_ref=src,
            dst_ref=dst,
            send_sem=s_sem,
            recv_sem=r_sem,
            device_id=target,
            device_id_type=MESH,
        )

    barrier = pltpu.get_barrier_semaphore()

    def greet_cp(n, carry):
        pl.semaphore_signal(barrier, inc=1, device_id=at_cp((c + n) % 16), device_id_type=MESH)
        return carry

    lax.fori_loop(1, 16, greet_cp, 0)
    for far in (1, 2, 3, 13, 14, 15):
        near = xl * 16 + (z + far) % 16
        pl.semaphore_signal(barrier, inc=1, device_id=(c, near), device_id_type=MESH)

    @pl.when(c // 8 != xl)
    def _():
        def greet_cross(n, carry):
            pl.semaphore_signal(barrier, inc=1, device_id=(n, cross), device_id_type=MESH)
            return carry

        lax.fori_loop(0, 16, greet_cross, 0)

    loads = []
    for n, (src, dst) in enumerate(
        (
            (q_in, q_ref),
            (k_in, k_ref),
            (v_in, v_ref),
            (do_in, do_ref),
            (o_in, o_ref),
            (ln_in, ln_ref),
            (lg_in, ring.at[z]),
            (gp_in, gp_ref),
            (id_in, id_ref),
            (hid_in.at[0], hid.at[c]),
        )
    ):
        copy = pltpu.make_async_copy(src, dst, in_s.at[n])
        copy.start()
        loads.append(copy)

    first = core == 0
    mine = pl.ds(pl.multiple_of(core * 128, 128), 128)
    lane = lax.broadcasted_iota(jnp.int32, (128, 128), 1)

    def stage():
        for copy in loads[0:6]:
            copy.wait()
        for side, (wide, narrow) in enumerate(((q_ref, do_ref), (k_ref, v_ref))):
            for ref, size, at in ((wide, QK, 0), (narrow, DH, QK)):
                turned = ref[...].T
                h0, h1 = turned[0:size], turned[size : 2 * size]
                own_t[side, at : at + size, mine] = jnp.where(first, h0, h1)
                sw_t[side, at : at + size, :] = jnp.where(first, h1, h0)
        prod = do_ref[...].astype(F32) * o_ref[...].astype(F32)
        d0 = jnp.sum(prod[:, 0:DH], axis=1, keepdims=True)
        d1 = jnp.sum(prod[:, DH : 2 * DH], axis=1, keepdims=True)
        rows_d = jnp.where(lane == 0, d0, jnp.where(lane == 1, d1, 0.0)).T[0:8, :]
        rows_n = ln_ref[...]
        sub = lax.broadcasted_iota(jnp.int32, (8, 128), 0)
        l0 = jnp.where(sub == 0, rows_n[0:1, :], rows_d[0:1, :])
        l1 = jnp.where(sub == 0, rows_n[1:2, :], rows_d[1:2, :])
        own_l[core] = jnp.where(first, l0, l1)
        sw_l[...] = jnp.where(first, l1, l0)

    def z_copy(back, far, n, rows, sem):
        block = (z + 16 + back) % 16
        ref = ring.at[block, rows, :]
        src = lg_in if back == 0 else ref
        target = xl * 16 + (z + 16 + far) % 16
        return remote(src, ref, rg_s.at[n], rg_r.at[block if sem is None else sem], (c, target))

    z_all = pl.ds(0, SHARE)
    z_half = (pl.ds(0, SHARE // 2), pl.ds(SHARE // 2, SHARE // 2))
    z_first = [z_copy(0, far, n, z_all, None) for n, far in enumerate((3, -3, 1, -1))]
    z_later = [
        [z_copy(-3, far, 4 + n, z_all, None) for n, far in enumerate((3, 1, -1))],
        [z_copy(3, far, 7 + n, z_all, None) for n, far in enumerate((-3, -1, 1))],
        [z_copy(-6, far, 10 + n, z_all, None) for n, far in enumerate((1, -1))]
        + [z_copy(-6, 2, 12, z_half[0], None)],
        [z_copy(6, far, 13 + n, z_all, None) for n, far in enumerate((-1, 1))]
        + [z_copy(6, -2, 15, z_half[1], 16)],
    ]

    def z_arrived(block, rows, sem):
        ref = ring.at[block, rows, :]
        remote(ref, ref, rg_s.at[0], rg_r.at[sem], at_cp(sib)).wait_recv()

    def z_pass(n):
        block = (z + (13, 3, 10, 6)[n]) % 16
        z_arrived(block, z_all, block)
        start(z_later[n])

    swaps = [
        remote(sw_t, own_t.at[:, :, mine], sw_s.at[0], sw_r.at[0], at_cp(sib)),
        remote(sw_l, own_l.at[core], sw_s.at[1], sw_r.at[1], at_cp(sib)),
    ]

    half_a, half_b = pl.ds(0, 32), pl.ds(32, 32)

    def ypeer(n):
        return (c + 4 * n) % 16

    def piece(owner, half):
        return hid.at[owner, half, :]

    def own_piece(n, target, half, col):
        return remote(
            hid_in.at[0, half, :], piece(c, half), ho_s.at[col, n], h_r.at[col, c], at_cp(target)
        )

    own_sends = [
        own_piece(n, target, half, col)
        for n, target, half, col in (
            (0, xpart, half_a, 0),
            (1, ypeer(1), half_a, 0),
            (3, ypeer(3), half_b, 1),
            (0, xpart, half_b, 1),
            (1, ypeer(1), half_b, 1),
            (3, ypeer(3), half_a, 0),
        )
    ]

    def att_copy(origin, source, rows, n, target):
        return (
            remote(source, far_t.at[origin], at_s.at[0, n], at_r.at[0, origin], at_cp(target)),
            remote(rows, far_l.at[origin], at_s.at[1, n], at_r.at[1, origin], at_cp(target)),
        )

    def att_own_copies(n, other):
        pick = jnp.where(other // 2 > chip, 1, 0)
        return att_copy(chip, own_t.at[pick], own_l, n, other)

    def att_passed(n):
        origin = (chip + 8 - 2 * n) % 8
        return att_copy(origin, far_t.at[origin], far_l.at[origin], 3 + n, xpart)

    def att_wait(origin):
        for copy in att_copy(origin, own_t.at[0], own_l, 0, sib):
            copy.wait_recv()

    def att_relay(n):
        att_wait((chip + 8 - 2 * n) % 8)
        start(att_passed(n))

    att_sends = [copy for n in (1, 3, 2) for copy in att_own_copies(n, (c + 4 * n) % 16)]
    att_sends += att_own_copies(0, xpart)
    whole = remote(hid_in.at[0], hid.at[c], ho_s.at[2, 0], h_r.at[2, c], at_cp(sib))

    def start(copies):
        for copy in copies:
            copy.start()

    def col_target(k):
        return xl * 8 + k

    def col_copy(k, n):
        return remote(
            send.at[k, n], cols.at[c], cl_s.at[k, n], cl_r.at[c], (col_target(k), n * 16 + z)
        )

    def dispatch(step, carry):
        k = (z // 2 + step + c // 4 + 2 * (c % 4)) % 8
        r0 = gate_0 * dot_nt(ring[2 * k], table_0)
        r1 = gate_1 * dot_nt(ring[2 * k + 1], table_1)
        for n, rows in enumerate((jnp.where(low, r0, r1), jnp.where(low, r1, r0))):
            send[k, n] = rows.astype(BF16)
            here = (col_target(k) == c) & (n == xl)

            @pl.when(here)
            def _():
                cols[c] = send[k, n]

            @pl.when(jnp.logical_not(here))
            def _():
                col_copy(k, n).start()

        return carry

    def dispatch_all():
        for far in (1, 15, 2, 14, 4, 12, 5, 11, 7, 9):
            z_arrived((z + far) % 16, z_all, (z + far) % 16)
        opposite = (z + 8) % 16
        z_arrived(opposite, z_half[0], opposite)
        z_arrived(opposite, z_half[1], 16)
        lax.fori_loop(0, 8, dispatch, 0)

    def joined(rows, n):
        return jnp.concatenate([rows[0, n : n + 1, :], rows[1, n : n + 1, :]], axis=1)

    def block(side, at, n, norm, delta, mask):
        a, b = at[n, 0:QK, :], at[n, QK:BOTH, :]
        probs = jnp.exp(SCALE * dot_nn(own_x[side], a) - norm)
        if mask is not None:
            probs = jnp.where(mask, probs, 0.0)
        ds = (probs * (dot_nn(own_y[side], b) - delta)).astype(BF16)
        return dot_nt(ds, a), dot_nt(probs.astype(BF16), b)

    def att_own():
        r_iota = lax.broadcasted_iota(jnp.int32, (256, 256), 0)
        c_iota = lax.broadcasted_iota(jnp.int32, (256, 256), 1)
        q_part, _ = block(0, own_t, 1, norm_col, delta_col, r_iota >= c_iota)
        k_part, v_part = block(1, own_t, 0, norm_row, delta_row, c_iota >= r_iota)
        acc_a[0] = q_part
        acc_a[1] = k_part
        acc_v[0] = jnp.zeros((256, DH), F32)
        acc_v[1] = v_part

    def att_step(other):
        side = jnp.where(other > chip, 1, 0)
        rows = far_l[other]
        is_far = other > chip
        norm = jnp.where(is_far, joined(rows, 0), norm_col)
        delta = jnp.where(is_far, joined(rows, 1), delta_col)
        part_a, part_v = block(side, far_t, other, norm, delta, None)
        acc_a[side] += part_a
        acc_v[side] += part_v

    def att_near(n, carry):
        att_step((chip + 8 - 2 * n) % 8)
        return carry

    def att_far(n, carry):
        other = (xpart // 2 + 8 - 2 * n) % 8
        att_wait(other)
        att_step(other)
        return carry

    sib_sends = []
    fwd_sends = []

    def arrived(owner, half, col):
        remote(
            piece(owner, half), piece(owner, half), hd_s.at[col, 0], h_r.at[col, owner], at_cp(sib)
        ).wait_recv()

    def to_sibling(owner, half, col, n):
        copy = remote(
            piece(owner, half), piece(owner, half), hd_s.at[col, n], h_r.at[col, owner], at_cp(sib)
        )
        copy.start()
        sib_sends.append(copy)

    def forward(owner, half, col, sem, target):
        copy = remote(piece(owner, half), piece(owner, half), sem, h_r.at[col, owner], at_cp(target))
        copy.start()
        fwd_sends.append(copy)

    def far_peer(n):
        return (xpart + 4 * n) % 16

    def relay_x(half, col):
        arrived(xpart, half, col)
        for n in (1, 3):
            forward(xpart, half, col, hb_s.at[2 * col + n // 2], ypeer(n))
        to_sibling(xpart, half, col, 0)

    def relay_y(n, near):
        owner = ypeer(n) if near else far_peer(n)
        half, col = (half_a, 0) if n == 3 else (half_b, 1)
        arrived(owner, half, col)
        forward(owner, half, col, ha_s.at[2 * near + col], ypeer(4 - n))
        to_sibling(owner, half, col, n + 4 * (1 - near))

    def keep_y(n, near, half, col):
        owner = ypeer(n) if near else far_peer(n)
        arrived(owner, half, col)
        to_sibling(owner, half, col, n + 4 * (1 - near))

    pl.semaphore_wait(barrier, 29)
    start(z_first)
    start(own_sends)
    stage()
    start(swaps)

    for copy in loads[6:]:
        copy.wait()
    ids = id_ref[...]
    gates = gp_ref[...]
    before_t = (lax.broadcasted_iota(jnp.int32, (128, 128), 0) < lane).astype(BF16)
    spots = lax.broadcasted_iota(jnp.int32, (CAP, 128), 0).astype(F32)
    tables, weights = [], []
    for n in range(2):
        hit = ids == 16 * n + z
        named = jnp.sum(jnp.where(hit, 1.0, 0.0), axis=0, keepdims=True)
        gate = jnp.sum(jnp.where(hit, gates, 0.0), axis=0, keepdims=True)
        earlier = dot_nn(jnp.broadcast_to(named, (8, 128)).astype(BF16), before_t)[0:1, :]
        inside = (spots == earlier) & (named > 0.5)
        tables.append(jnp.where(inside, 1.0, 0.0))
        weights.append(jnp.where(inside, gate, 0.0))
    table_0 = jnp.concatenate(tables, axis=0).astype(BF16)
    table_1 = jnp.concatenate(tables[::-1], axis=0).astype(BF16)
    gate_0 = jnp.sum(jnp.concatenate(weights, axis=0).T, axis=0, keepdims=True)
    gate_1 = jnp.sum(jnp.concatenate(weights[::-1], axis=0).T, axis=0, keepdims=True)
    low = lax.broadcasted_iota(jnp.int32, (SHARE, 128), 1) < CAP

    for copy in swaps:
        copy.wait_recv()
    start(att_sends)
    start([whole])
    z_pass(0)
    z_pass(1)
    relay_x(half_a, 0)
    relay_x(half_b, 1)
    relay_y(3, 1)
    z_pass(2)
    z_pass(3)
    relay_y(1, 1)
    att_relay(1)
    att_relay(3)
    att_relay(2)
    relay_y(3, 0)
    relay_y(1, 0)
    for side in range(2):
        own_x[side] = own_t[side, 0:QK, :].T
        own_y[side] = own_t[side, QK:BOTH, :].T

    own_rows = own_l[...]
    norm_row, delta_row = joined(own_rows, 0), joined(own_rows, 1)
    turned_l = [
        jnp.concatenate([own_rows[n], jnp.zeros((120, 128), F32)], axis=0).T for n in range(2)
    ]
    norm_col = jnp.concatenate([turned_l[0][:, 0:1], turned_l[1][:, 0:1]], axis=0)
    delta_col = jnp.concatenate([turned_l[0][:, 1:2], turned_l[1][:, 1:2]], axis=0)
    att_own()
    lax.fori_loop(1, 4, att_near, 0)
    dispatch_all()
    lax.fori_loop(0, 4, att_far, 0)
    theirs = pl.ds(pl.multiple_of((1 - core) * 128, 128), 128)
    for n in range(2):
        fo_a[n] = (SCALE * acc_a[n, theirs, :]).astype(BF16)
    fo_b[...] = acc_v[1, theirs, :].astype(BF16)
    backs = [
        remote(fo_a, fi_a, fo_s.at[0], fo_r.at[0], at_cp(sib)),
        remote(fo_b, fi_b, fo_s.at[1], fo_r.at[1], at_cp(sib)),
    ]
    for copy in backs:
        copy.start()
    for near in (1, 0):
        keep_y(1, near, half_a, 0)
        keep_y(3, near, half_b, 1)
        keep_y(2, near, half_a, 0)
        keep_y(2, near, half_b, 1)

    for copy in backs:
        copy.wait()
    for n, ref in enumerate((qg_ref, kg_ref)):
        kept = (SCALE * acc_a[n, mine, :]).astype(BF16)
        got = fi_a[n]
        ref[:, 0:QK] = jnp.where(first, kept, got)
        ref[:, QK : 2 * QK] = jnp.where(first, got, kept)
    kept = acc_v[1, mine, :].astype(BF16)
    got = fi_b[...]
    vg_ref[:, 0:DH] = jnp.where(first, kept, got)
    vg_ref[:, DH : 2 * DH] = jnp.where(first, got, kept)

    remote(hid.at[sib], hid.at[sib], ho_s.at[2, 0], h_r.at[2, sib], at_cp(sib)).wait_recv()

    def from_sibling(n, carry):
        owner = (sib + 2 * n) % 16
        arrived(owner, half_a, 0)
        arrived(owner, half_b, 1)
        return carry

    lax.fori_loop(1, 8, from_sibling, 0)

    def col_wait(n, carry):
        @pl.when(jnp.logical_not((n == c) & (c // 8 == xl)))
        def _():
            remote(send.at[0, 0], cols.at[n], cl_s.at[0, 0], cl_r.at[n], at_cp(sib)).wait_recv()

        return carry

    lax.fori_loop(0, 16, col_wait, 0)

    for m in range(8):
        p0, p1 = cols[2 * m], cols[2 * m + 1]
        t0 = jnp.concatenate([p0[:, 0:CAP], p1[:, 0:CAP]], axis=1)
        t1 = jnp.concatenate([p0[:, CAP : 2 * CAP], p1[:, CAP : 2 * CAP]], axis=1)
        left[0:SHARE, 128 * m : 128 * m + 128] = jnp.where(xl == 0, t0, t1)
        left[SHARE : 2 * SHARE, 128 * m : 128 * m + 128] = jnp.where(xl == 0, t1, t0)

    for copy in swaps + own_sends + fwd_sends + sib_sends + [whole] + att_sends + z_first + sum(z_later, []):
        copy.wait_send()

    for n in (1, 2, 3):
        for copy in att_passed(n):
            copy.wait_send()

    def cols_sent(k, carry):
        for n in range(2):

            @pl.when(jnp.logical_not((col_target(k) == c) & (n == xl)))
            def _():
                col_copy(k, n).wait_send()

        return carry

    lax.fori_loop(0, 8, cols_sent, 0)


def product(left, hid, q_in, k_in, v_in, q_out, k_out, v_out, out):
    right = hid[...].reshape(16 * CAP, hid.shape[2])
    out[0] = dot_nn(left[...], right).astype(BF16)

    @pl.when(pl.program_id(0) == 0)
    def _():
        q_out[...] = q_in[...]
        k_out[...] = k_in[...]
        v_out[...] = v_in[...]


def local(q, k, v, do, o, ln, lg, gp, ids, hidden):
    vmem = pl.BlockSpec(memory_space=pltpu.VMEM)
    hbm = pl.BlockSpec(memory_space=pltpu.HBM)
    dma = pltpu.SemaphoreType.DMA
    shapes = (
        jax.ShapeDtypeStruct((128, 2 * QK), BF16),
        jax.ShapeDtypeStruct((128, 2 * QK), BF16),
        jax.ShapeDtypeStruct((128, 2 * DH), BF16),
    )
    q_part, k_part, v_part, left, rows = pl.pallas_call(
        kernel,
        out_shape=shapes
        + (
            jax.ShapeDtypeStruct((2 * SHARE, 16 * CAP), BF16),
            jax.ShapeDtypeStruct((16, CAP, 2048), BF16),
        ),
        in_specs=[hbm] * 10,
        out_specs=(vmem,) * 4 + (hbm,),
        scratch_shapes=[
            pltpu.VMEM((128, 2 * QK), BF16),
            pltpu.VMEM((128, 2 * QK), BF16),
            pltpu.VMEM((128, 2 * DH), BF16),
            pltpu.VMEM((128, 2 * DH), BF16),
            pltpu.VMEM((128, 2 * DH), BF16),
            pltpu.VMEM((2, 128), F32),
            pltpu.VMEM((8, 128), F32),
            pltpu.VMEM((8, 128), jnp.int32),
            pltpu.VMEM((2, BOTH, 256), BF16),
            pltpu.VMEM((2, 256, QK), BF16),
            pltpu.VMEM((2, 256, DH), BF16),
            pltpu.VMEM((2, 8, 128), F32),
            pltpu.VMEM((2, BOTH, 128), BF16),
            pltpu.VMEM((8, 128), F32),
            pltpu.VMEM((8, BOTH, 256), BF16),
            pltpu.VMEM((8, 2, 8, 128), F32),
            pltpu.VMEM((2, 256, QK), F32),
            pltpu.VMEM((2, 256, DH), F32),
            pltpu.VMEM((2, 128, QK), BF16),
            pltpu.VMEM((128, DH), BF16),
            pltpu.VMEM((2, 128, QK), BF16),
            pltpu.VMEM((128, DH), BF16),
            pltpu.VMEM((16, SHARE, 128), BF16),
            pltpu.VMEM((8, 2, SHARE, 128), BF16),
            pltpu.VMEM((16, SHARE, 128), BF16),
            dma((10,)),
            dma((2,)),
            dma((2,)),
            dma((2, 8)),
            dma((2, 8)),
            dma((2,)),
            dma((2,)),
            dma((16,)),
            dma((17,)),
            dma((8, 2)),
            dma((16,)),
            dma((3, 4)),
            dma((4,)),
            dma((4,)),
            dma((2, 8)),
            dma((3, 16)),
        ],
        compiler_params=pltpu.CompilerParams(
            collective_id=0, has_side_effects=True, vmem_limit_bytes=60 * 2**20
        ),
    )(q, k, v, do, o, ln, lg.T, gp.T, ids.T, hidden)
    def whole(*shape):
        return pl.BlockSpec(shape, lambda n: (0,) * len(shape))

    grads = [whole(128, 2 * QK), whole(128, 2 * QK), whole(128, 2 * DH)]
    q_grad, k_grad, v_grad, down = pl.pallas_call(
        product,
        grid=(4,),
        out_shape=shapes + (jax.ShapeDtypeStruct((1, 2 * SHARE, 2048), BF16),),
        in_specs=[
            whole(2 * SHARE, 16 * CAP),
            pl.BlockSpec((16, CAP, 2048 // 4), lambda n: (0, 0, n)),
        ]
        + grads,
        out_specs=tuple(grads)
        + (pl.BlockSpec((1, 2 * SHARE, 2048 // 4), lambda n: (0, 0, n)),),
        compiler_params=pltpu.CompilerParams(vmem_limit_bytes=60 * 2**20),
    )(left, rows, q_part, k_part, v_part)
    return q_grad, k_grad, v_grad, jnp.swapaxes(down, 1, 2)


def solution(mesh):
    return jax.shard_map(
        local,
        mesh=mesh,
        in_specs=(
            P("cp", "ep"),
            P("cp", "ep"),
            P("cp", "ep"),
            P("cp", "ep"),
            P("cp", "ep"),
            P("ep", "cp"),
            P("cp", "ep"),
            P("cp", None),
            P("cp", None),
            P("ep", "cp", None),
        ),
        out_specs=(P("cp", "ep"), P("cp", "ep"), P("cp", "ep"), P("ep", None, "cp")),
        check_vma=False,
    )
```
